128 devices in a mesh: fold: 8 (over y, x_hi), col: 16 (over z, x_lo, core).
Axes of the slice: x: 4 (x_hi: 2, x_lo: 2; x = x_hi * 2 + x_lo), y: 4, z: 4, core: 2. Of those that a mesh axis runs over, the one named last changes fastest.
Arguments:
- bin_embed: bfloat16 [48, 2048], P(None, 'col'), may hold values from -6 to 6
- conv_weight: bfloat16 [9, 48, 48], replicated, may hold values from -0.3125 to 0.3125
- conv_bias: float32 [48], replicated, may hold values from -3 to 3
- dilation: int32 [2], replicated, may hold values from 1 to 16, as said below
- fold_map: int32 [128, 2], replicated, may hold values from 0 to 15, as said below
- cotangent: bfloat16 [8, 16, 48, 128, 128], P('fold', 'col'), may hold values from -6 to 6
Outputs:
- pair_out: bfloat16 [8, 16, 48, 128, 128], P('fold', 'col')
- grad_embed: float32 [48, 2048], P(None, 'col')
- grad_weight: float32 [9, 48, 48], replicated
- grad_bias: float32 [48], replicated
The draws below stay inside these ranges and needn't reach their ends.
Inputs may be any that keep to these rules, and one draw needn't show every extreme that they name: `dilation`: one rate is exactly 16, the other is smaller; which one is drawn. `fold_map`: rows are tile pairs below 16. Every pair i < j appears once; every pair (i, j) with i > j and i + j = 15 appears once; nothing else. The order is random.
All inputs are finite; a program needn't handle non-finite values.
Results may differ from the reference program's by a relative error of at most 0.0047.
Values may be sent and summed in bfloat16 or wider, within the bound.
No kernel may reach another device: no remote copies, remote signals or barrier semaphores. Data moves between devices by JAX's collectives and lax.ppermute only.
A program may use at most 192 MiB of HBM per device.

```python
import jax
import jax.numpy as jnp
import numpy as np
from jax import lax

C = 48
B = 128
DMAX = 16
TILES = 16
L = 2048
N_FOLD = 8
N_COL = 16


def draw_dilation(key, part):
    key = jax.random.fold_in(key, 11)
    smaller_rate = jax.random.randint(jax.random.fold_in(key, 1), (), 1, DMAX)
    swap_flag = jax.random.randint(jax.random.fold_in(key, 2), (), 0, 2)
    largest = jnp.int32(DMAX)
    return jnp.where(swap_flag == 0, jnp.stack([largest, smaller_rate]), jnp.stack([smaller_rate, largest])).astype(jnp.int32)


def draw_fold_map(key, part):
    key = jax.random.fold_in(key, 7)
    pair_list = []
    for upper_tile in range(TILES):
        for other_tile in range(upper_tile + 1, TILES):
            pair_list.append((upper_tile, other_tile))
    for lower_tile in range(TILES // 2):
        pair_list.append((TILES - 1 - lower_tile, lower_tile))
    pair_table = jnp.array(np.array(pair_list, dtype=np.int32))
    shuffle = jax.random.permutation(key, pair_table.shape[0])
    return pair_table[shuffle].astype(jnp.int32)


def levels(own_key, dims, shards, low, high):
    level, own = 1.0, jax.random.fold_in(own_key, 6)
    for axis_at, parts in shards:
        heights = jnp.exp(jax.random.uniform(jax.random.fold_in(own, axis_at), (parts,), jnp.float32, low / len(shards), high / len(shards)))
        level = level * jnp.repeat(heights, dims[axis_at] // parts).reshape([-1 if axis == axis_at else 1 for axis in range(len(dims))])
    return level


def normal_values(stream_key, shape, deviation, reach, split=(), kind=jnp.bfloat16):
    level = levels(stream_key, shape, split, -0.22, 0.18) if split else 1.0
    drawn = jax.random.normal(stream_key, shape, jnp.float32) * deviation * level
    return jnp.minimum(jnp.maximum(drawn, -reach), reach).astype(kind)


def setup_inputs(seed: int = 0) -> dict:
    streams_of = jax.random.split(jax.random.key(seed), 7)
    bin_embed = normal_values(streams_of[0], (C, L), 1.0, 6.0, ((1, 16),))
    conv_weight = normal_values(streams_of[1], (9, C, C), (9 * C) ** -0.5, 0.3125)
    conv_bias = normal_values(streams_of[2], (C,), 0.5, 3.0, (), jnp.float32)
    dilation = draw_dilation(jax.random.fold_in(streams_of[6], 71), 0)
    fold_map = draw_fold_map(jax.random.fold_in(streams_of[6], 71), 0)
    cotangent = normal_values(streams_of[5], (N_FOLD, N_COL, C, B, B), 1.0, 6.0, ((0, 8), (1, 16)))
    return {"bin_embed": bin_embed, "conv_weight": conv_weight, "conv_bias": conv_bias, "dilation": dilation, "fold_map": fold_map, "cotangent": cotangent}


tap_rows = (-1, -1, -1, 0, 0, 0, 1, 1, 1)
tap_cols = (-1, 0, 1, -1, 0, 1, -1, 0, 1)


def build_tile(padded_embed, padded_valid, row_index, col_index, tile_width):
    extent = tile_width + 2 * DMAX
    row_values = lax.dynamic_slice_in_dim(padded_embed, row_index * tile_width, extent, 1)
    col_values = lax.dynamic_slice_in_dim(padded_embed, col_index * tile_width, extent, 1)
    row_live = lax.dynamic_slice_in_dim(padded_valid, row_index * tile_width, extent, 0)
    col_live = lax.dynamic_slice_in_dim(padded_valid, col_index * tile_width, extent, 0)
    pre_act = row_values[:, :, None] + col_values[:, None, :]
    open_mask = (pre_act > 0).astype(jnp.float32) * (row_live[:, None] * col_live[None, :])[None]
    return (pre_act * open_mask).astype(jnp.bfloat16), open_mask


def conv_forward(activity, weight, dilation, tile_width):
    channels = activity.shape[0]
    summed = jnp.zeros((weight.shape[2], tile_width, tile_width), jnp.float32)
    for tap_index in range(9):
        start_row = DMAX + tap_rows[tap_index] * dilation[0]
        start_col = DMAX + tap_cols[tap_index] * dilation[1]
        window = lax.dynamic_slice(activity, (jnp.int32(0), start_row, start_col), (channels, tile_width, tile_width))
        summed = summed + jnp.einsum("io,irs->ors", weight[tap_index].astype(jnp.float32), window.astype(jnp.float32))
    return summed


def conv_backward(activity, open_mask, grad_tile, weight, dilation, tile_width):
    channels = activity.shape[0]
    grad_ext = jnp.zeros(activity.shape, jnp.float32)
    grad_float = grad_tile.astype(jnp.float32)
    tap_grads = []
    for tap_index in range(9):
        start_row = DMAX + tap_rows[tap_index] * dilation[0]
        start_col = DMAX + tap_cols[tap_index] * dilation[1]
        window = lax.dynamic_slice(activity, (jnp.int32(0), start_row, start_col), (channels, tile_width, tile_width))
        tap_grads.append(jnp.einsum("irs,ors->io", window.astype(jnp.float32), grad_float))
        contrib = jnp.einsum("io,ors->irs", weight[tap_index].astype(jnp.float32), grad_float)
        region = lax.dynamic_slice(grad_ext, (jnp.int32(0), start_row, start_col), (channels, tile_width, tile_width))
        grad_ext = lax.dynamic_update_slice(grad_ext, region + contrib, (jnp.int32(0), start_row, start_col))
    grad_pre = grad_ext * open_mask
    return jnp.sum(grad_pre, axis=2), jnp.sum(grad_pre, axis=1), jnp.stack(tap_grads), jnp.sum(grad_float, axis=(1, 2))


def add_block(partial_value, piece, offset):
    region = lax.dynamic_slice_in_dim(partial_value, offset, piece.shape[1], 1)
    return lax.dynamic_update_slice_in_dim(partial_value, region + piece, offset, 1)


def tile_step(padded_embed, padded_valid, weight, bias, dilation, tile_pair, cot_tile, tile_width):
    row_index = tile_pair[0]
    col_index = tile_pair[1]
    channels = weight.shape[1]
    span = padded_embed.shape[1]

    def one_tile():
        activity, open_mask = build_tile(padded_embed, padded_valid, row_index, col_index, tile_width)
        summed = conv_forward(activity, weight, dilation, tile_width) + bias[:, None, None]
        row_part, col_part, weight_grad, bias_grad = conv_backward(activity, open_mask, cot_tile, weight, dilation, tile_width)
        partial_value = jnp.zeros((channels, span), jnp.float32)
        partial_value = add_block(partial_value, row_part, row_index * tile_width)
        partial_value = add_block(partial_value, col_part, col_index * tile_width)
        return summed.astype(jnp.bfloat16), partial_value, weight_grad, bias_grad

    def two_tiles():
        act_high, mask_high = build_tile(padded_embed, padded_valid, row_index, row_index, tile_width)
        act_low, mask_low = build_tile(padded_embed, padded_valid, col_index, col_index, tile_width)
        out_high = conv_forward(act_high, weight, dilation, tile_width) + bias[:, None, None]
        out_low = conv_forward(act_low, weight, dilation, tile_width) + bias[:, None, None]
        line = lax.broadcasted_iota(jnp.int32, (tile_width, tile_width), 0)
        column = lax.broadcasted_iota(jnp.int32, (tile_width, tile_width), 1)
        upper_mask = (column >= line)[None]
        merged = jnp.where(upper_mask, out_high, jnp.swapaxes(out_low, 1, 2))
        zero_tile = jnp.zeros_like(cot_tile)
        grad_high = jnp.where(upper_mask, cot_tile, zero_tile)
        grad_low = jnp.swapaxes(jnp.where(upper_mask, zero_tile, cot_tile), 1, 2)
        rows_high, cols_high, wgrad_high, bgrad_high = conv_backward(act_high, mask_high, grad_high, weight, dilation, tile_width)
        rows_low, cols_low, wgrad_low, bgrad_low = conv_backward(act_low, mask_low, grad_low, weight, dilation, tile_width)
        partial_value = jnp.zeros((channels, span), jnp.float32)
        partial_value = add_block(partial_value, rows_high, row_index * tile_width)
        partial_value = add_block(partial_value, cols_high, row_index * tile_width)
        partial_value = add_block(partial_value, rows_low, col_index * tile_width)
        partial_value = add_block(partial_value, cols_low, col_index * tile_width)
        return merged.astype(jnp.bfloat16), partial_value, wgrad_high + wgrad_low, bgrad_high + bgrad_low

    return lax.cond(row_index > col_index, two_tiles, one_tile)


def reference(bin_embed, conv_weight, conv_bias, dilation, fold_map, cotangent):
    channels, bin_count = bin_embed.shape
    tile_width = cotangent.shape[-1]
    padded_embed = jnp.pad(bin_embed.astype(jnp.float32), ((0, 0), (DMAX, DMAX)))
    padded_valid = jnp.pad(jnp.ones((bin_count,), jnp.float32), (DMAX, DMAX))
    cot_tiles = cotangent.reshape((-1, channels, tile_width, tile_width))

    def visit(totals, inputs_now):
        tile_pair, cot_tile = inputs_now
        tile_out, partial_value, weight_grad, bias_grad = tile_step(padded_embed, padded_valid, conv_weight, conv_bias, dilation, tile_pair, cot_tile, tile_width)
        return (totals[0] + partial_value, totals[1] + weight_grad, totals[2] + bias_grad), tile_out

    initial = (jnp.zeros((channels, bin_count + 2 * DMAX), jnp.float32), jnp.zeros(conv_weight.shape, jnp.float32), jnp.zeros((channels,), jnp.float32))
    sums_out, tiles_out = lax.scan(visit, initial, (fold_map, cot_tiles))
    pair_out = tiles_out.reshape(cotangent.shape)
    grad_embed = sums_out[0][:, DMAX:DMAX + bin_count] * (bin_count ** -0.5)
    return pair_out, grad_embed, sums_out[1] / bin_count, sums_out[2] / bin_count
```

```python
import functools

import jax
import jax.numpy as jnp
import numpy as np
from jax import lax
from jax.experimental import pallas as pl
from jax.experimental.pallas import tpu as pltpu
from jax.sharding import PartitionSpec as P

C = 48
B = 128
DMAX = 16
NK = 448
OUTSIDE = -16384.0
F32 = jnp.float32
BF16 = jnp.bfloat16
UNROLL = 8
ROWS = 4
VMEM_BYTES = 48 * 1024 * 1024

NT = (((1,), (1,)), ((), ()))
TN = (((0,), (0,)), ((), ()))
NN = (((1,), (0,)), ((), ()))


def dot(a, b, dims):
    return lax.dot_general(a, b, dims, preferred_element_type=F32)


def repeat_table():
    table = np.zeros((2, 144, NK), np.float32)
    for u in range(3):
        for v in range(3):
            for i in range(C):
                column = (3 * u + v) * C + i
                table[0, u * C + i, column] = 1.0
                table[1, v * C + i, column] = 1.0
    return jnp.asarray(table, BF16)


def fill_blocks(meta, own, core, xlo, z1, z2, z3, blocks):
    z, x, c = meta[4], meta[5], meta[6]
    blocks[0] = jnp.full((C, B), OUTSIDE, F32)
    blocks[17] = jnp.full((C, B), OUTSIDE, F32)
    blocks[1 + z * 4 + x * 2 + c] = own[...].astype(F32)
    blocks[1 + z * 4 + x * 2 + (1 - c)] = core[...].astype(F32)
    blocks[1 + z * 4 + (1 - x) * 2 + c] = xlo[0].astype(F32)
    blocks[1 + z * 4 + (1 - x) * 2 + (1 - c)] = xlo[1].astype(F32)
    for step, got in ((1, z1), (2, z2), (3, z3)):
        zz = z ^ step
        blocks[1 + zz * 4 + x * 2 + c] = got[0].astype(F32)
        blocks[1 + zz * 4 + x * 2 + (1 - c)] = got[1].astype(F32)
        blocks[1 + zz * 4 + (1 - x) * 2 + c] = got[2].astype(F32)
        blocks[1 + zz * 4 + (1 - x) * 2 + (1 - c)] = got[3].astype(F32)


def spread_lanes(blocks, tile, table):
    before, here, after = blocks[tile], blocks[tile + 1], blocks[tile + 2]
    for q in range(-DMAX, B + DMAX):
        source, lane = (before, q + B) if q < 0 else ((here, q) if q < B else (after, q - B))
        table[DMAX + q] = jnp.broadcast_to(source[:, lane : lane + 1], (C, B)).astype(BF16)


def windows(blocks, tile, rate):
    lane = lax.broadcasted_iota(jnp.int32, (C, B), 1)
    before, here, after = blocks[tile], blocks[tile + 1], blocks[tile + 2]
    low = jnp.where(lane < rate, pltpu.roll(before, rate, 1), pltpu.roll(here, rate, 1))
    high = jnp.where(lane >= B - rate, pltpu.roll(after, B - rate, 1), pltpu.roll(here, B - rate, 1))
    return [low.astype(BF16), here.astype(BF16), high.astype(BF16)]


def scatter_back(grads, tile, rate, shifted):
    lane = lax.broadcasted_iota(jnp.int32, (C, B), 1)
    low, here, high = shifted
    low = pltpu.roll(low, B - rate, 1)
    high = pltpu.roll(high, rate, 1)
    zero = jnp.zeros((C, B), F32)
    grads[tile] += jnp.where(lane >= B - rate, low, zero)
    grads[tile + 2] += jnp.where(lane < rate, high, zero)
    grads[tile + 1] += (
        jnp.where(lane < B - rate, low, zero) + here + jnp.where(lane >= rate, high, zero)
    )


def backward_kernel(
    meta, own, core, xlo, z1, z2, z3, cot_rows, cot_cols, weight, repeat,
    send, keep,
    blocks, table_i, table_j, shift, sums, grads, wgrad,
):
    tile_i, tile_j, rate_r, rate_c, core_index = meta[0], meta[1], meta[2], meta[3], meta[6]
    fill_blocks(meta, own, core, xlo, z1, z2, z3, blocks)
    spread_lanes(blocks, tile_i, table_i)
    spread_lanes(blocks, tile_j, table_j)
    one, zero = jnp.ones((), BF16), jnp.zeros((), BF16)
    bias_rows = jnp.ones((NK - 432, B), BF16)
    column = lax.broadcasted_iota(jnp.int32, (B, NK), 1)
    bias_mark = jnp.where(column == 432, 1.0, 0.0)
    grads[...] = jnp.zeros_like(grads)

    def shifts_of(slot, window, which, mark):
        table = dot(jnp.concatenate(window, 0), repeat[which], TN)
        shift[slot] = table + bias_mark if mark else table

    def back_sums(slot, tile, rate, which):
        total = sums[slot]
        high = total.astype(BF16)
        low = (total - high.astype(F32)).astype(BF16)
        merged = dot(repeat[which], high, NT) + dot(repeat[which], low, NT)
        scatter_back(grads, tile, rate, [merged[k * C : (k + 1) * C] for k in range(3)])

    def each(step):
        def several(outer, carry):
            for inner in range(UNROLL):
                carry = step(outer * UNROLL + inner, carry)
            return carry
        return several

    weight_now = weight[...]

    def take(slot, q, products, total):
        sums[slot, pl.ds(q, 1), :] = jnp.sum(products * weight_now, axis=0, keepdims=True)
        return total + products * shift[slot, pl.ds(q, 1), :]

    empty = jnp.zeros((C, NK), F32)

    @pl.when(tile_i < tile_j)
    def one_tile():
        window_i, window_j = windows(blocks, tile_i, rate_r), windows(blocks, tile_j, rate_c)
        shifts_of(0, window_i, 0, True)
        shifts_of(1, window_j, 1, False)
        minus_i, minus_j = [-w for w in window_i], [-w for w in window_j]

        def row(q, total):
            at = [table_i[DMAX + q + k * rate_r] for k in (-1, 0, 1)]
            mask = [jnp.where(at[u] > minus_j[v], one, zero) for u in range(3) for v in range(3)]
            return take(0, q, dot(cot_rows[q], jnp.concatenate(mask + [bias_rows], 0), NT), total)

        def col(q, total):
            at = [table_j[DMAX + q + k * rate_c] for k in (-1, 0, 1)]
            mask = [jnp.where(at[v] > minus_i[u], one, zero) for u in range(3) for v in range(3)]
            return take(1, q, dot(cot_cols[q], jnp.concatenate(mask + [bias_rows], 0), NT), total)

        total = lax.fori_loop(0, B // UNROLL, each(row), empty)
        wgrad[...] = lax.fori_loop(0, B // UNROLL, each(col), total)
        back_sums(0, tile_i, rate_r, 0)
        back_sums(1, tile_j, rate_c, 1)

    @pl.when(tile_i > tile_j)
    def two_triangles():
        up_r, up_c = windows(blocks, tile_i, rate_r), windows(blocks, tile_i, rate_c)
        low_r, low_c = windows(blocks, tile_j, rate_r), windows(blocks, tile_j, rate_c)
        shifts_of(0, up_r, 0, True)
        shifts_of(1, up_c, 1, False)
        shifts_of(2, low_c, 1, True)
        shifts_of(3, low_r, 0, False)
        lane = lax.broadcasted_iota(jnp.int32, (C, B), 1)

        def both(q, total, cot, upper, up, up_window, low, low_window, slot):
            mask = []
            for u in range(3):
                for v in range(3):
                    at = jnp.where(upper, up(u, v), low(u, v))
                    other = jnp.where(upper, up_window(u, v), low_window(u, v))
                    mask.append(jnp.where(at > other, one, zero))
            mask = jnp.concatenate(mask + [bias_rows], 0)
            none = jnp.zeros_like(cot)
            parts = jnp.concatenate([jnp.where(upper, cot, none), jnp.where(upper, none, cot)], 0)
            products = dot(parts, mask, NT)
            total = take(slot, q, products[:C], total)
            return take(slot + 2, q, products[C:], total)

        m_up_r, m_up_c = [-w for w in up_r], [-w for w in up_c]
        m_low_r, m_low_c = [-w for w in low_r], [-w for w in low_c]

        def row(q, total):
            up = [table_i[DMAX + q + k * rate_r] for k in (-1, 0, 1)]
            low = [table_j[DMAX + q + k * rate_c] for k in (-1, 0, 1)]
            return both(
                q, total, cot_rows[q], lane >= q,
                lambda u, v: up[u], lambda u, v: m_up_c[v],
                lambda u, v: low[v], lambda u, v: m_low_r[u], 0,
            )

        def col(q, total):
            up = [table_i[DMAX + q + k * rate_c] for k in (-1, 0, 1)]
            low = [table_j[DMAX + q + k * rate_r] for k in (-1, 0, 1)]
            return both(
                q, total, cot_cols[q], lane <= q,
                lambda u, v: up[v], lambda u, v: m_up_r[u],
                lambda u, v: low[u], lambda u, v: m_low_c[v], 1,
            )

        total = lax.fori_loop(0, B // UNROLL, each(row), empty)
        wgrad[...] = lax.fori_loop(0, B // UNROLL, each(col), total)
        back_sums(0, tile_i, rate_r, 0)
        back_sums(1, tile_i, rate_c, 1)
        back_sums(2, tile_j, rate_c, 1)
        back_sums(3, tile_j, rate_r, 0)

    for pair in range(8):
        send[pair] = grads[1 + 2 * pair + (1 - core_index)].astype(BF16)
        keep[pair] = grads[1 + 2 * pair + core_index].astype(BF16)
    total = wgrad[...]
    for part in range(4):
        piece = total[:, part * B : min((part + 1) * B, NK)].astype(BF16)
        if piece.shape[1] < B:
            piece = jnp.concatenate([piece, jnp.zeros((C, B - piece.shape[1]), BF16)], 1)
        send[8 + part] = piece
        keep[8 + part] = piece


def forward_kernel(
    meta, own, core, xlo, z1, z2, z3, weight, bias, out, blocks, table_i, table_j
):
    tile_i, tile_j, rate_r, rate_c = meta[0], meta[1], meta[2], meta[3]
    fill_blocks(meta, own, core, xlo, z1, z2, z3, blocks)
    spread_lanes(blocks, tile_i, table_i)
    weight_now = weight[...]
    bias_now = bias[...]
    zero = jnp.zeros((), BF16)

    def finish(first, parts):
        full = dot(weight_now, jnp.concatenate(parts, 1), NN)
        for k in range(ROWS):
            out[first + k] = (full[:, k * B : (k + 1) * B] + bias_now).astype(BF16)

    @pl.when(tile_i < tile_j)
    def one_tile():
        window = windows(blocks, tile_j, rate_c)

        def some(step, carry):
            parts = []
            for k in range(ROWS):
                q = step * ROWS + k
                at = [table_i[DMAX + q + m * rate_r] for m in (-1, 0, 1)]
                parts.append(
                    jnp.concatenate(
                        [jnp.maximum(at[u] + window[v], zero) for u in range(3) for v in range(3)], 0
                    )
                )
            finish(step * ROWS, parts)
            return carry

        lax.fori_loop(0, B // ROWS, some, 0)

    @pl.when(tile_i > tile_j)
    def two_triangles():
        spread_lanes(blocks, tile_j, table_j)
        up_window, low_window = windows(blocks, tile_i, rate_c), windows(blocks, tile_j, rate_r)
        lane = lax.broadcasted_iota(jnp.int32, (C, B), 1)

        def some(step, carry):
            parts = []
            for k in range(ROWS):
                q = step * ROWS + k
                upper = lane >= q
                up = [table_i[DMAX + q + m * rate_r] for m in (-1, 0, 1)]
                low = [table_j[DMAX + q + m * rate_c] for m in (-1, 0, 1)]
                parts.append(
                    jnp.concatenate(
                        [
                            jnp.maximum(
                                jnp.where(upper, up[u] + up_window[v], low[v] + low_window[u]), zero
                            )
                            for u in range(3)
                            for v in range(3)
                        ],
                        0,
                    )
                )
            finish(step * ROWS, parts)
            return carry

        lax.fori_loop(0, B // ROWS, some, 0)


def shape(dims, kind):
    return jax.ShapeDtypeStruct(dims, kind)


def call(kernel, out_shape, n_in, scratch=(), **cost):
    specs = [pl.BlockSpec(memory_space=pltpu.SMEM)] + [pl.BlockSpec(memory_space=pltpu.VMEM)] * n_in
    return pl.pallas_call(
        kernel,
        out_shape=out_shape,
        in_specs=specs,
        scratch_shapes=list(scratch),
        compiler_params=pltpu.CompilerParams(vmem_limit_bytes=VMEM_BYTES),
        cost_estimate=pl.CostEstimate(**cost) if cost else None,
    )


def backward(meta, pieces, cot_rows, cot_cols, weight, repeat):
    return call(
        backward_kernel,
        (shape((12, C, B), BF16), shape((12, C, B), BF16)),
        len(pieces) + 4,
        [
            pltpu.VMEM((18, C, B), F32),
            pltpu.VMEM((B + 2 * DMAX, C, B), BF16),
            pltpu.VMEM((B + 2 * DMAX, C, B), BF16),
            pltpu.VMEM((4, B, NK), F32),
            pltpu.VMEM((4, B, NK), F32),
            pltpu.VMEM((18, C, B), F32),
            pltpu.VMEM((C, NK), F32),
        ],
        flops=2 * 2 * B * B * C * NK, bytes_accessed=4 * B * B * C, transcendentals=0,
    )(meta, *pieces, cot_rows, cot_cols, weight, repeat)


def forward(meta, pieces, weight, bias):
    return call(
        forward_kernel,
        shape((B, C, B), BF16),
        len(pieces) + 2,
        [
            pltpu.VMEM((18, C, B), F32),
            pltpu.VMEM((B + 2 * DMAX, C, B), BF16),
            pltpu.VMEM((B + 2 * DMAX, C, B), BF16),
        ],
        flops=2 * B * B * C * 432, bytes_accessed=2 * B * B * C, transcendentals=0,
    )(meta, *pieces, weight, bias)


def after_core_kernel(meta, keep, got, own, to1, to2, to3):
    z = meta[4]
    total = [keep[k].astype(F32) + got[k].astype(F32) for k in range(8, 12)]
    for step, out in ((0, own), (1, to1), (2, to2), (3, to3)):
        first = (z ^ step) * 2
        for k in range(2):
            out[k] = (keep[first + k].astype(F32) + got[first + k].astype(F32)).astype(BF16)
        for k in range(4):
            out[2 + k] = total[k].astype(BF16)


def sum4(own, a, b, c, k):
    return (own[k].astype(F32) + a[k].astype(F32)) + (b[k].astype(F32) + c[k].astype(F32))


def after_z_kernel(meta, keep, a, b, c, own, other):
    x = meta[5]
    own[0] = sum4(keep, a, b, c, x).astype(BF16)
    other[0] = sum4(keep, a, b, c, 1 - x).astype(BF16)
    for k in range(4):
        total = sum4(keep, a, b, c, 2 + k).astype(BF16)
        own[1 + k] = total
        other[1 + k] = total


def after_x_kernel(meta, keep, a, b, c, own):
    for k in range(5):
        own[k] = sum4(keep, a, b, c, k).astype(BF16)


def after_y_kernel(meta, keep, a, b, c, grad_embed, grad_weight, grad_bias):
    grad_embed[...] = sum4(keep, a, b, c, 0) * (2048.0**-0.5)
    total = jnp.concatenate([sum4(keep, a, b, c, 1 + k) for k in range(4)], 1) * (1.0 / 2048.0)
    turned = total.T
    grad_weight[...] = turned[:432].reshape(9, C, C)
    grad_bias[...] = turned[432:440]


def body(bin_embed, conv_weight, conv_bias, dilation, fold_map, cotangent):
    fold, col = lax.axis_index("fold"), lax.axis_index("col")
    pair = lax.dynamic_slice_in_dim(fold_map, fold * 16 + col, 1, 0)[0]
    meta = jnp.concatenate([pair, dilation, jnp.stack([col // 4, (col // 2) % 2, col % 2])])

    def swap(value, fold_bits, col_bits):
        route = [
            (f * 16 + c, (f ^ fold_bits) * 16 + (c ^ col_bits)) for f in range(8) for c in range(16)
        ]
        return lax.ppermute(value, ("fold", "col"), route)

    core = swap(bin_embed, 0, 1)
    pair_blocks = jnp.stack([bin_embed, core])
    xlo = swap(pair_blocks, 0, 2)
    quad = jnp.concatenate([pair_blocks, xlo], 0)
    z1, z2, z3 = (swap(quad, 0, 4 * step) for step in (1, 2, 3))
    pieces = (bin_embed, core, xlo, z1, z2, z3)

    cot = cotangent[0, 0]
    cot_rows = jnp.transpose(cot, (1, 0, 2))
    cot_cols = jnp.transpose(cot, (2, 0, 1))
    flat = jnp.transpose(conv_weight, (2, 0, 1)).reshape(C, 432)
    weight = jnp.pad(flat.astype(F32), ((0, 0), (0, NK - 432)))
    bias = jnp.broadcast_to(conv_bias[:, None], (C, B))

    send, keep = backward(meta, pieces, cot_rows, cot_cols, weight, repeat_table())
    got = swap(send, 0, 1)
    half = shape((6, C, B), BF16)
    keep, to1, to2, to3 = call(after_core_kernel, (half,) * 4, 2)(meta, keep, got)
    a, b, c = swap(to1, 0, 4), swap(to2, 0, 8), swap(to3, 0, 12)
    part = shape((5, C, B), BF16)
    keep, other = call(after_z_kernel, (part, part), 4)(meta, keep, a, b, c)
    a, b, c = swap(other, 0, 2), swap(keep, 1, 0), swap(other, 1, 2)
    keep = call(after_x_kernel, part, 4)(meta, keep, a, b, c)
    a, b, c = swap(keep, 2, 0), swap(keep, 4, 0), swap(keep, 6, 0)
    grad_embed, grad_weight, grad_bias = call(
        after_y_kernel, (shape((C, B), F32), shape((9, C, C), F32), shape((8, C), F32)), 4
    )(meta, keep, a, b, c)
    pair_out = jnp.transpose(forward(meta, pieces, flat, bias), (1, 0, 2))
    return pair_out[None, None], grad_embed, grad_weight, grad_bias[0]


def solution(mesh):
    placed = (P(None, "col"), P(), P(), P(), P(), P("fold", "col", None, None, None))
    return jax.shard_map(
        body,
        mesh=mesh,
        in_specs=placed,
        out_specs=(P("fold", "col", None, None, None), P(None, "col"), P(), P()),
        check_vma=False,
    )
```

```python
import functools

import jax
import jax.numpy as jnp
import numpy as np
from jax import lax
from jax.experimental import pallas as pl
from jax.experimental.pallas import tpu as pltpu
from jax.sharding import PartitionSpec as P

C = 48
B = 128
DMAX = 16
NK = 512
OUTSIDE = -16384.0
F32 = jnp.float32
BF16 = jnp.bfloat16
UNROLL = 16
PARTS = 4
ROWS = 32
PAD = 8
PIECES = ((0, 48), (48, 48), (96, 32))
VMEM_BYTES = 48 * 1024 * 1024

NT = (((1,), (1,)), ((), ()))
TN = (((0,), (0,)), ((), ()))
NN = (((1,), (0,)), ((), ()))


def dot(a, b, dims):
    return lax.dot_general(a, b, dims, preferred_element_type=F32)


def repeat_table():
    table = np.zeros((2, 144, NK), np.float32)
    for u in range(3):
        for v in range(3):
            for i in range(C):
                column = (3 * u + v) * C + i
                table[0, u * C + i, column] = 1.0
                table[1, v * C + i, column] = 1.0
    return jnp.asarray(table, BF16)


def fill_blocks(meta, own, core, xlo, both, z1, z2, z3, blocks):
    z, x, c = meta[4], meta[5], meta[6]
    blocks[0] = jnp.full((C, B), OUTSIDE, F32)
    blocks[17] = jnp.full((C, B), OUTSIDE, F32)
    here = 1 + z * 4
    blocks[here + x * 2 + c] = own[...].astype(F32)
    blocks[here + x * 2 + (1 - c)] = core[...].astype(F32)
    blocks[here + (1 - x) * 2 + c] = xlo[...].astype(F32)
    blocks[here + (1 - x) * 2 + (1 - c)] = both[...].astype(F32)
    for step, got in ((1, z1), (2, z2), (3, z3)):
        there = 1 + (z ^ step) * 4
        blocks[there + x * 2 + c] = got[0].astype(F32)
        blocks[there + x * 2 + (1 - c)] = got[1].astype(F32)
        blocks[there + (1 - x) * 2 + c] = got[2].astype(F32)
        blocks[there + (1 - x) * 2 + (1 - c)] = got[3].astype(F32)


def spread_lanes(blocks, tile, table, first, count):
    before, here, after = blocks[tile], blocks[tile + 1], blocks[tile + 2]
    for q in range(first - DMAX, first + count + DMAX):
        source, lane = (before, q + B) if q < 0 else ((here, q) if q < B else (after, q - B))
        table[q - first + DMAX] = jnp.broadcast_to(source[:, lane : lane + 1], (C, B)).astype(BF16)


def windows(blocks, tile, rate):
    lane = lax.broadcasted_iota(jnp.int32, (C, B), 1)
    before, here, after = blocks[tile], blocks[tile + 1], blocks[tile + 2]
    low = jnp.where(lane < rate, pltpu.roll(before, rate, 1), pltpu.roll(here, rate, 1))
    high = jnp.where(lane >= B - rate, pltpu.roll(after, B - rate, 1), pltpu.roll(here, B - rate, 1))
    return [low.astype(BF16), here.astype(BF16), high.astype(BF16)]


def scatter_back(grads, tile, rate, shifted):
    lane = lax.broadcasted_iota(jnp.int32, (C, B), 1)
    low, here, high = shifted
    low = pltpu.roll(low, B - rate, 1)
    high = pltpu.roll(high, rate, 1)
    zero = jnp.zeros((C, B), F32)
    grads[tile] += jnp.where(lane >= B - rate, low, zero)
    grads[tile + 2] += jnp.where(lane < rate, high, zero)
    grads[tile + 1] += (
        jnp.where(lane < B - rate, low, zero) + here + jnp.where(lane >= rate, high, zero)
    )


def bias_lanes(bias):
    return jnp.broadcast_to(bias[...], (B, C)).T


def store_rows(full, bias, first, stage32, count):
    for k in range(full.shape[1] // B):
        stage32[pl.ds(first + k, C, stride=count + PAD), :] = full[:, k * B : (k + 1) * B] + bias


def round_rows(stage32, stage, count):
    for c in range(C):
        stage[c] = stage32[c * (count + PAD) : c * (count + PAD) + count, :].astype(BF16)


def gradient_kernel(
    meta, own, core, xlo, both, z1, z2, z3, conv_weight, conv_bias, repeat, cot_hbm, cols_hbm,
    send, keep, around, pair_hbm,
    blocks, shift, minus, sums, grads, wgrad, table, cot, rows, cols, cot32, stage32, stage, sems,
):
    tile_i, tile_j, rate_r, rate_c, core_index = meta[0], meta[1], meta[2], meta[3], meta[6]
    load_cot = pltpu.make_async_copy(cot_hbm, cot, sems.at[0])
    load_cols = pltpu.make_async_copy(cols_hbm, cols, sems.at[1])
    load_cot.start()
    load_cols.start()
    fill_blocks(meta, own, core, xlo, both, z1, z2, z3, blocks)
    for k in range(3):
        around[k] = blocks[tile_i + k]
        around[3 + k] = blocks[tile_j + k]
    one, zero = jnp.ones((), BF16), jnp.zeros((), BF16)
    column = lax.broadcasted_iota(jnp.int32, (B, NK), 1)
    bias_mark = jnp.where(column == 432, 1.0, 0.0)
    grads[...] = jnp.zeros_like(grads)
    weight = conv_weight[...].astype(F32).T
    weight_wide = jnp.concatenate([weight, jnp.zeros((C, NK - 432), F32)], 1)
    empty = jnp.zeros((C, NK), F32)

    def tables(slot, tile, rate, which, mark):
        table = dot(jnp.concatenate(windows(blocks, tile, rate), 0), repeat[which], TN)
        minus[slot] = (-table).astype(BF16)
        shift[slot] = table + bias_mark if mark else table

    def back_sums(slot, tile, rate, which):
        tiles = []
        for at in range(NK // B):
            total = sums[slot, at, pl.ds(0, B, stride=8), :]
            for part in range(1, 8):
                total += sums[slot, at, pl.ds(part, B, stride=8), :]
            tiles.append(total)
        total = jnp.concatenate(tiles, 1)
        high = total.astype(BF16)
        low = (total - high.astype(F32)).astype(BF16)
        merged = dot(repeat[which], high, NT) + dot(repeat[which], low, NT)
        scatter_back(grads, tile, rate, [merged[k * C : (k + 1) * C] for k in range(3)])

    def loop(steps, start, first=0, last=B):
        def several(outer, carry):
            for inner in range(UNROLL):
                for step in steps:
                    carry = step(outer * UNROLL + inner, carry)
            return carry

        return lax.fori_loop(first // UNROLL, last // UNROLL, several, start)

    def take(slot, q, products, total):
        weighted = products * weight_wide
        partial = weighted[:8]
        for part in range(1, C // 8):
            partial += weighted[8 * part : 8 * part + 8]
        for at in range(NK // B):
            sums[slot, at, pl.ds(pl.multiple_of(q * 8, 8), 8), :] = partial[:, at * B : (at + 1) * B]
        return total + products * shift[slot, pl.ds(q, 1), :]

    def row_of(q):
        return rows[q]

    def col_of(q):
        return cols[q]

    def cotangent_here():
        load_cot.wait()
        for c in range(C):
            cot32[c * (B + PAD) : c * (B + PAD) + B, :] = cot[c].astype(F32)
        for q in range(B):
            rows[q] = cot32[pl.ds(q, C, stride=B + PAD), :].astype(BF16)
        load_cols.wait()

    @pl.when(tile_i < tile_j)
    def one_tile():
        spread_lanes(blocks, tile_i, table, 0, B)
        bias, short = bias_lanes(conv_bias), weight.astype(BF16)
        window = windows(blocks, tile_j, rate_c)

        def some(step, carry):
            parts = []
            for k in range(ROWS):
                at = [table[DMAX + step * ROWS + k + m * rate_r] for m in (-1, 0, 1)]
                taps = [jnp.maximum(at[u] + window[v], zero) for u in range(3) for v in range(3)]
                parts.append(jnp.concatenate(taps, 0))
            store_rows(dot(short, jnp.concatenate(parts, 1), NN), bias, step * ROWS, stage32, B)
            return carry

        lax.fori_loop(0, B // ROWS, some, 0)
        round_rows(stage32, stage, B)
        save_pair = pltpu.make_async_copy(stage, pair_hbm, sems.at[2])
        save_pair.start()

        tables(0, tile_i, rate_r, 0, True)
        tables(1, tile_j, rate_c, 1, False)
        cotangent_here()

        def half(slot, other, grad_of):
            def step(q, total):
                at = jnp.broadcast_to(shift[slot, pl.ds(q, 1), :], (16, NK)).astype(BF16)
                at = jnp.concatenate([at] * (B // 16), 0)
                mask = jnp.where(at > minus[other], one, zero)
                return take(slot, q, dot(grad_of(q), mask, NN), total)

            return step

        wgrad[...] = loop([half(0, 1, row_of), half(1, 0, col_of)], empty)
        back_sums(0, tile_i, rate_r, 0)
        back_sums(1, tile_j, rate_c, 1)
        save_pair.wait()

    @pl.when(tile_i > tile_j)
    def two_triangles():
        tables(0, tile_i, rate_r, 0, True)
        tables(1, tile_i, rate_c, 1, False)
        tables(2, tile_j, rate_c, 1, True)
        tables(3, tile_j, rate_r, 0, False)
        cotangent_here()
        lane = lax.broadcasted_iota(jnp.int32, (C, B), 1).astype(BF16)

        def half(slot, other, grad_of, side, live):
            def step(q, total):
                at = jnp.broadcast_to(shift[slot, pl.ds(q, 1), :], (16, NK)).astype(BF16)
                at = jnp.concatenate([at] * ((live.stop - live.start) // 16), 0)
                mask = jnp.where(at > minus[other, live, :], one, zero)
                pads = [jnp.zeros((n, NK), BF16) for n in (live.start, B - live.stop)]
                mask = jnp.concatenate([x for x in (pads[0], mask, pads[1]) if x.shape[0]], 0)
                place = jnp.full((C, B), q, F32).astype(BF16)
                grad = jnp.where(side(lane, place), grad_of(q), zero)
                return take(slot, q, dot(grad, mask, NN), total)

            return step

        total = empty
        for part in range(PARTS):
            lines = (part * B // PARTS, (part + 1) * B // PARTS)
            after, before = slice(lines[0], B), slice(0, lines[1])
            total = loop(
                [
                    half(0, 1, row_of, lambda s, r: s >= r, after),
                    half(1, 0, col_of, lambda r, s: r <= s, before),
                    half(2, 3, row_of, lambda s, r: s < r, before),
                    half(3, 2, col_of, lambda r, s: r > s, after),
                ],
                total,
                *lines,
            )
        wgrad[...] = total
        back_sums(0, tile_i, rate_r, 0)
        back_sums(1, tile_i, rate_c, 1)
        back_sums(2, tile_j, rate_c, 1)
        back_sums(3, tile_j, rate_r, 0)

    for pair in range(8):
        send[pair] = grads[1 + 2 * pair + (1 - core_index)]
        keep[pair] = grads[1 + 2 * pair + core_index]
    total = wgrad[...]
    for part in range(4):
        piece = total[:, part * B : (part + 1) * B]
        send[8 + part] = piece
        keep[8 + part] = piece


def fold_kernel(
    first, count, meta, around, conv_weight, conv_bias, pair_before, after, pair_hbm, token,
    table_i, table_j, stage32, stage, sem,
):
    tile_i, tile_j, rate_r, rate_c = meta[0], meta[1], meta[2], meta[3]
    token[...] = jnp.zeros_like(token)

    @pl.when(tile_i > tile_j)
    def two_triangles():
        spread_lanes(around, 0, table_i, first, count)
        spread_lanes(around, 3, table_j, first, count)
        up_window, low_window = windows(around, 0, rate_c), windows(around, 3, rate_r)
        lane = lax.broadcasted_iota(jnp.int32, (C, B), 1)
        bias, short = bias_lanes(conv_bias), conv_weight[...].astype(F32).T.astype(BF16)
        zero = jnp.zeros((), BF16)

        def some(step, carry):
            parts = []
            for k in range(16):
                q = step * 16 + k
                upper = lane >= first + q
                up = [table_i[DMAX + q + m * rate_r] for m in (-1, 0, 1)]
                low = [table_j[DMAX + q + m * rate_c] for m in (-1, 0, 1)]
                taps = [
                    jnp.where(upper, up[u] + up_window[v], low[v] + low_window[u])
                    for u in range(3)
                    for v in range(3)
                ]
                parts.append(jnp.concatenate([jnp.maximum(x, zero) for x in taps], 0))
            store_rows(dot(short, jnp.concatenate(parts, 1), NN), bias, step * 16, stage32, count)
            return carry

        lax.fori_loop(0, count // 16, some, 0)
        round_rows(stage32, stage, count)
        save = pltpu.make_async_copy(stage, pair_hbm.at[:, pl.ds(first, count), :], sem)
        save.start()
        save.wait()


def shape(dims, kind):
    return jax.ShapeDtypeStruct(dims, kind)


SMEM = pl.BlockSpec(memory_space=pltpu.SMEM)
VMEM = pl.BlockSpec(memory_space=pltpu.VMEM)
ANY = pl.BlockSpec(memory_space=pl.ANY)


def call(kernel, in_specs, out_shape, out_specs, scratch=(), aliases={}):
    return pl.pallas_call(
        kernel,
        out_shape=out_shape,
        in_specs=in_specs,
        out_specs=out_specs,
        scratch_shapes=list(scratch),
        input_output_aliases=aliases,
        compiler_params=pltpu.CompilerParams(vmem_limit_bytes=VMEM_BYTES),
    )


def gradients(meta, pieces, conv_weight, conv_bias, cot, cot_cols):
    return call(
        gradient_kernel,
        [SMEM] + [VMEM] * (len(pieces) + 3) + [ANY, ANY],
        (shape((12, C, B), F32), shape((12, C, B), F32), shape((6, C, B), F32), shape((C, B, B), BF16)),
        (VMEM, VMEM, VMEM, ANY),
        [
            pltpu.VMEM((18, C, B), F32),
            pltpu.VMEM((4, B, NK), F32),
            pltpu.VMEM((4, B, NK), BF16),
            pltpu.VMEM((4, NK // B, 8 * B, B), F32),
            pltpu.VMEM((18, C, B), F32),
            pltpu.VMEM((C, NK), F32),
            pltpu.VMEM((B + 2 * DMAX, C, B), BF16),
            pltpu.VMEM((C, B, B), BF16),
            pltpu.VMEM((B, C, B), BF16),
            pltpu.VMEM((B, C, B), BF16),
            pltpu.VMEM((C * (B + PAD), B), F32),
            pltpu.VMEM((C * (B + PAD), B), F32),
            pltpu.VMEM((C, B, B), BF16),
            pltpu.SemaphoreType.DMA((3,)),
        ],
    )(meta, *pieces, conv_weight, conv_bias, repeat_table(), cot, cot_cols)


def fold(which, meta, around, conv_weight, conv_bias, pair, after):
    first, count = PIECES[which]
    return call(
        functools.partial(fold_kernel, first, count),
        [SMEM, VMEM, VMEM, VMEM, ANY, ANY],
        (shape((C, B, B), BF16), shape((8, B), F32)),
        (ANY, VMEM),
        [
            pltpu.VMEM((count + 2 * DMAX, C, B), BF16),
            pltpu.VMEM((count + 2 * DMAX, C, B), BF16),
            pltpu.VMEM((C * (count + PAD), B), F32),
            pltpu.VMEM((C, count, B), BF16),
            pltpu.SemaphoreType.DMA,
        ],
        {4: 0},
    )(meta, around, conv_weight, conv_bias, pair, after)


def after_core_kernel(meta, keep, got, own, to1, to2, to3):
    z = meta[4]
    total = [(keep[k] + got[k]).astype(BF16) for k in range(8, 12)]
    for step, out in ((0, own), (1, to1), (2, to2), (3, to3)):
        first = (z ^ step) * 2
        for k in range(2):
            out[k] = (keep[first + k] + got[first + k]).astype(BF16)
        for k in range(4):
            out[2 + k] = total[k]


def sum4(own, a, b, c, k):
    return (own[k].astype(F32) + a[k].astype(F32)) + (b[k].astype(F32) + c[k].astype(F32))


def after_z_kernel(meta, keep, a, b, c, token, own, other):
    x = meta[5]
    own[0] = sum4(keep, a, b, c, x).astype(BF16)
    other[0] = sum4(keep, a, b, c, 1 - x).astype(BF16)
    for k in range(4):
        total = sum4(keep, a, b, c, 2 + k).astype(BF16)
        own[1 + k] = total
        other[1 + k] = total


def after_x_kernel(meta, keep, a, b, c, token, own):
    for k in range(5):
        own[k] = sum4(keep, a, b, c, k).astype(BF16)


def after_y_kernel(meta, keep, a, b, c, grad_embed, grad_weight, grad_bias):
    grad_embed[...] = sum4(keep, a, b, c, 0) * (2048.0**-0.5)
    total = jnp.concatenate([sum4(keep, a, b, c, 1 + k) for k in range(4)], 1) * (1.0 / 2048.0)
    turned = total.T
    grad_weight[...] = turned[:432].reshape(9, C, C)
    grad_bias[...] = turned[432:433]


def body(bin_embed, conv_weight, conv_bias, dilation, fold_map, cotangent):
    fold_at, col = lax.axis_index("fold"), lax.axis_index("col")
    pair = lax.dynamic_slice_in_dim(fold_map, fold_at * 16 + col, 1, 0)[0]
    meta = jnp.concatenate([pair, dilation, jnp.stack([col // 4, (col // 2) % 2, col % 2])])

    def swap(value, fold_bits, col_bits):
        route = [
            (f * 16 + c, (f ^ fold_bits) * 16 + (c ^ col_bits)) for f in range(8) for c in range(16)
        ]
        return lax.ppermute(value, ("fold", "col"), route)

    core, xlo, both = swap(bin_embed, 0, 1), swap(bin_embed, 0, 2), swap(bin_embed, 0, 3)
    quad = jnp.stack([bin_embed, core, xlo, both])
    z1, z2, z3 = (swap(quad, 0, 4 * step) for step in (1, 2, 3))
    pieces = (bin_embed, core, xlo, both, z1, z2, z3)

    cot = cotangent[0, 0]
    cot_cols = jnp.transpose(cot, (2, 0, 1))
    weight, bias = conv_weight.reshape(9 * C, C), conv_bias.reshape(1, C)
    send, keep, around, pair_out = gradients(meta, pieces, weight, bias, cot, cot_cols)

    def next_rows(which, pair_out, after):
        return fold(which, meta, around, weight, bias, pair_out, after)

    got = swap(send, 0, 1)
    half, part = shape((6, C, B), BF16), shape((5, C, B), BF16)
    keep, to1, to2, to3 = call(
        after_core_kernel, [SMEM, VMEM, VMEM], (half,) * 4, (VMEM,) * 4
    )(meta, keep, got)
    pair_out, token = next_rows(0, pair_out, keep)
    a, b, c = swap(to1, 0, 4), swap(to2, 0, 8), swap(to3, 0, 12)
    keep, other = call(
        after_z_kernel, [SMEM] + [VMEM] * 4 + [ANY], (part, part), (VMEM, VMEM)
    )(meta, keep, a, b, c, token)
    pair_out, token = next_rows(1, pair_out, keep)
    a, b, c = swap(other, 0, 2), swap(keep, 1, 0), swap(other, 1, 2)
    keep = call(after_x_kernel, [SMEM] + [VMEM] * 4 + [ANY], part, VMEM)(meta, keep, a, b, c, token)
    pair_out, token = next_rows(2, pair_out, keep)
    a, b, c = swap(keep, 2, 0), swap(keep, 4, 0), swap(keep, 6, 0)
    grad_embed, grad_weight, grad_bias = call(
        after_y_kernel,
        [SMEM] + [VMEM] * 4,
        (shape((C, B), F32), shape((9, C, C), F32), shape((1, C), F32)),
        (VMEM,) * 3,
    )(meta, keep, a, b, c)
    return pair_out[None, None], grad_embed, grad_weight, grad_bias.reshape(C)


def solution(mesh):
    placed = (P(None, "col"), P(), P(), P(), P(), P("fold", "col", None, None, None))
    return jax.shard_map(
        body,
        mesh=mesh,
        in_specs=placed,
        out_specs=(P("fold", "col", None, None, None), P(None, "col"), P(), P()),
        check_vma=False,
    )
```

```python
import functools

import jax
import jax.numpy as jnp
import numpy as np
from jax import lax
from jax.experimental import pallas as pl
from jax.experimental.pallas import tpu as pltpu
from jax.sharding import PartitionSpec as P

C = 48
B = 128
DMAX = 16
NK = 512
OUTSIDE = -16384.0
F32 = jnp.float32
BF16 = jnp.bfloat16
UNROLL = 16
PARTS = 4
ROWS = 32
PAD = 8
PIECES = ((0, 48), (48, 48), (96, 32))
VMEM_BYTES = 48 * 1024 * 1024

NT = (((1,), (1,)), ((), ()))
TN = (((0,), (0,)), ((), ()))
NN = (((1,), (0,)), ((), ()))


def dot(a, b, dims):
    return lax.dot_general(a, b, dims, preferred_element_type=F32)


def repeat_table():
    table = np.zeros((2, 144, NK), np.float32)
    for u in range(3):
        for v in range(3):
            for i in range(C):
                column = (3 * u + v) * C + i
                table[0, u * C + i, column] = 1.0
                table[1, v * C + i, column] = 1.0
    return jnp.asarray(table, BF16)


def position():
    return lax.axis_index("fold"), lax.axis_index("col")


def tile_of(fold_map, dilation):
    fold, col = position()
    slot = fold * 16 + col
    return fold_map[0, slot], fold_map[1, slot], dilation[0], dilation[1]


def place_of():
    col = position()[1]
    return col // 4, (col // 2) % 2, col % 2


def quad_kernel(own, core, xlo, both, out):
    for k, block in enumerate((own, core, xlo, both)):
        out[k] = block[...]


def fill_blocks(quad, z1, z2, z3, blocks):
    z, x, c = place_of()
    blocks[0] = jnp.full((C, B), OUTSIDE, F32)
    blocks[17] = jnp.full((C, B), OUTSIDE, F32)
    for step, got in ((0, quad), (1, z1), (2, z2), (3, z3)):
        there = 1 + (z ^ step) * 4
        for k in range(4):
            blocks[there + (x ^ (k // 2)) * 2 + (c ^ (k % 2))] = got[k].astype(F32)


def spread_lanes(blocks, tile, table, first, count):
    before, here, after = blocks[tile], blocks[tile + 1], blocks[tile + 2]
    for q in range(first - DMAX, first + count + DMAX):
        source, lane = (before, q + B) if q < 0 else ((here, q) if q < B else (after, q - B))
        table[q - first + DMAX] = jnp.broadcast_to(source[:, lane : lane + 1], (C, B)).astype(BF16)


def windows(blocks, tile, rate):
    lane = lax.broadcasted_iota(jnp.int32, (C, B), 1)
    before, here, after = blocks[tile], blocks[tile + 1], blocks[tile + 2]
    low = jnp.where(lane < rate, pltpu.roll(before, rate, 1), pltpu.roll(here, rate, 1))
    high = jnp.where(lane >= B - rate, pltpu.roll(after, B - rate, 1), pltpu.roll(here, B - rate, 1))
    return [low.astype(BF16), here.astype(BF16), high.astype(BF16)]


def scatter_back(grads, tile, rate, shifted):
    lane = lax.broadcasted_iota(jnp.int32, (C, B), 1)
    low, here, high = shifted
    low = pltpu.roll(low, B - rate, 1)
    high = pltpu.roll(high, rate, 1)
    zero = jnp.zeros((C, B), F32)
    grads[tile] += jnp.where(lane >= B - rate, low, zero)
    grads[tile + 2] += jnp.where(lane < rate, high, zero)
    grads[tile + 1] += (
        jnp.where(lane < B - rate, low, zero) + here + jnp.where(lane >= rate, high, zero)
    )


def bias_lanes(bias):
    return jnp.broadcast_to(bias[...], (B, C)).T


def store_rows(full, bias, first, stage32, count):
    for k in range(full.shape[1] // B):
        stage32[pl.ds(first + k, C, stride=count + PAD), :] = full[:, k * B : (k + 1) * B] + bias


def round_rows(stage32, stage, count):
    for c in range(C):
        stage[c] = stage32[c * (count + PAD) : c * (count + PAD) + count, :].astype(BF16)


def gradient_kernel(
    fold_map, dilation, quad, z1, z2, z3, conv_weight, repeat, bias_hbm, cot_hbm, cols_hbm,
    send, keep, around, pair_hbm,
    blocks, shift, minus, sums, grads, wgrad, table, cot, rows, cols, cot32, stage32, stage, bias_row, sems,
):
    tile_i, tile_j, rate_r, rate_c = tile_of(fold_map, dilation)
    core_index = place_of()[2]
    load_bias = pltpu.make_async_copy(bias_hbm, bias_row, sems.at[3])
    load_bias.start()
    load_cot = pltpu.make_async_copy(cot_hbm, cot, sems.at[0])
    load_cols = pltpu.make_async_copy(cols_hbm, cols, sems.at[1])
    load_cot.start()
    load_cols.start()
    fill_blocks(quad, z1, z2, z3, blocks)
    load_bias.wait()
    for k in range(3):
        around[k] = blocks[tile_i + k]
        around[3 + k] = blocks[tile_j + k]
    one, zero = jnp.ones((), BF16), jnp.zeros((), BF16)
    column = lax.broadcasted_iota(jnp.int32, (B, NK), 1)
    bias_mark = jnp.where(column == 432, 1.0, 0.0)
    grads[...] = jnp.zeros_like(grads)
    weight = conv_weight[...].astype(F32).T
    weight_wide = jnp.concatenate([weight, jnp.zeros((C, NK - 432), F32)], 1)
    empty = jnp.zeros((C, NK), F32)

    def tables(slot, tile, rate, which, mark):
        table = dot(jnp.concatenate(windows(blocks, tile, rate), 0), repeat[which], TN)
        minus[slot] = (-table).astype(BF16)
        shift[slot] = table + bias_mark if mark else table

    def back_sums(slot, tile, rate, which):
        tiles = []
        for at in range(NK // B):
            total = sums[slot, at, pl.ds(0, B, stride=8), :]
            for part in range(1, 8):
                total += sums[slot, at, pl.ds(part, B, stride=8), :]
            tiles.append(total)
        total = jnp.concatenate(tiles, 1)
        high = total.astype(BF16)
        low = (total - high.astype(F32)).astype(BF16)
        merged = dot(repeat[which], high, NT) + dot(repeat[which], low, NT)
        scatter_back(grads, tile, rate, [merged[k * C : (k + 1) * C] for k in range(3)])

    def loop(steps, start, first=0, last=B):
        def several(outer, carry):
            for inner in range(UNROLL):
                for step in steps:
                    carry = step(outer * UNROLL + inner, carry)
            return carry

        return lax.fori_loop(first // UNROLL, last // UNROLL, several, start)

    def take(slot, q, products, total):
        weighted = products * weight_wide
        partial = weighted[:8]
        for part in range(1, C // 8):
            partial += weighted[8 * part : 8 * part + 8]
        for at in range(NK // B):
            sums[slot, at, pl.ds(pl.multiple_of(q * 8, 8), 8), :] = partial[:, at * B : (at + 1) * B]
        return total + products * shift[slot, pl.ds(q, 1), :]

    def row_of(q):
        return rows[q]

    def col_of(q):
        return cols[q]

    def cotangent_here():
        load_cot.wait()
        for c in range(C):
            cot32[c * (B + PAD) : c * (B + PAD) + B, :] = cot[c].astype(F32)
        for q in range(B):
            rows[q] = cot32[pl.ds(q, C, stride=B + PAD), :].astype(BF16)
        load_cols.wait()

    @pl.when(tile_i < tile_j)
    def one_tile():
        spread_lanes(blocks, tile_i, table, 0, B)
        bias, short = bias_lanes(bias_row), weight.astype(BF16)
        window = windows(blocks, tile_j, rate_c)

        def some(step, carry):
            parts = []
            for k in range(ROWS):
                at = [table[DMAX + step * ROWS + k + m * rate_r] for m in (-1, 0, 1)]
                taps = [jnp.maximum(at[u] + window[v], zero) for u in range(3) for v in range(3)]
                parts.append(jnp.concatenate(taps, 0))
            store_rows(dot(short, jnp.concatenate(parts, 1), NN), bias, step * ROWS, stage32, B)
            return carry

        lax.fori_loop(0, B // ROWS, some, 0)
        round_rows(stage32, stage, B)
        save_pair = pltpu.make_async_copy(stage, pair_hbm, sems.at[2])
        save_pair.start()

        tables(0, tile_i, rate_r, 0, True)
        tables(1, tile_j, rate_c, 1, False)
        cotangent_here()

        def half(slot, other, grad_of):
            def step(q, total):
                at = jnp.broadcast_to(shift[slot, pl.ds(q, 1), :], (16, NK)).astype(BF16)
                at = jnp.concatenate([at] * (B // 16), 0)
                mask = jnp.where(at > minus[other], one, zero)
                return take(slot, q, dot(grad_of(q), mask, NN), total)

            return step

        wgrad[...] = loop([half(0, 1, row_of), half(1, 0, col_of)], empty)
        back_sums(0, tile_i, rate_r, 0)
        back_sums(1, tile_j, rate_c, 1)
        save_pair.wait()

    @pl.when(tile_i > tile_j)
    def two_triangles():
        tables(0, tile_i, rate_r, 0, True)
        tables(1, tile_i, rate_c, 1, False)
        tables(2, tile_j, rate_c, 1, True)
        tables(3, tile_j, rate_r, 0, False)
        cotangent_here()
        lane = lax.broadcasted_iota(jnp.int32, (C, B), 1).astype(BF16)

        def half(slot, other, grad_of, side, live):
            def step(q, total):
                at = jnp.broadcast_to(shift[slot, pl.ds(q, 1), :], (16, NK)).astype(BF16)
                at = jnp.concatenate([at] * ((live.stop - live.start) // 16), 0)
                mask = jnp.where(at > minus[other, live, :], one, zero)
                pads = [jnp.zeros((n, NK), BF16) for n in (live.start, B - live.stop)]
                mask = jnp.concatenate([x for x in (pads[0], mask, pads[1]) if x.shape[0]], 0)
                place = jnp.full((C, B), q, F32).astype(BF16)
                grad = jnp.where(side(lane, place), grad_of(q), zero)
                return take(slot, q, dot(grad, mask, NN), total)

            return step

        total = empty
        for part in range(PARTS):
            lines = (part * B // PARTS, (part + 1) * B // PARTS)
            after, before = slice(lines[0], B), slice(0, lines[1])
            total = loop(
                [
                    half(0, 1, row_of, lambda s, r: s >= r, after),
                    half(1, 0, col_of, lambda r, s: r <= s, before),
                    half(2, 3, row_of, lambda s, r: s < r, before),
                    half(3, 2, col_of, lambda r, s: r > s, after),
                ],
                total,
                *lines,
            )
        wgrad[...] = total
        back_sums(0, tile_i, rate_r, 0)
        back_sums(1, tile_i, rate_c, 1)
        back_sums(2, tile_j, rate_c, 1)
        back_sums(3, tile_j, rate_r, 0)

    for pair in range(8):
        send[pair] = grads[1 + 2 * pair + (1 - core_index)]
        keep[pair] = grads[1 + 2 * pair + core_index]
    total = wgrad[...]
    for part in range(4):
        piece = total[:, part * B : (part + 1) * B]
        send[8 + part] = piece
        keep[8 + part] = piece


def fold_kernel(
    first, count, fold_map, dilation, around, conv_weight, bias_hbm, pair_before, after,
    pair_hbm, token,
    table_i, table_j, stage32, stage, bias_row, sems,
):
    tile_i, tile_j, rate_r, rate_c = tile_of(fold_map, dilation)
    token[...] = jnp.zeros_like(token)

    @pl.when(tile_i > tile_j)
    def two_triangles():
        load_bias = pltpu.make_async_copy(bias_hbm, bias_row, sems.at[0])
        load_bias.start()
        spread_lanes(around, 0, table_i, first, count)
        spread_lanes(around, 3, table_j, first, count)
        up_window, low_window = windows(around, 0, rate_c), windows(around, 3, rate_r)
        lane = lax.broadcasted_iota(jnp.int32, (C, B), 1).astype(BF16)
        short = conv_weight[...].astype(F32).T.astype(BF16)
        load_bias.wait()
        bias, zero = bias_lanes(bias_row), jnp.zeros((), BF16)
        saves = []
        for chunk in range(count // 16):
            parts = []
            for k in range(16):
                q = chunk * 16 + k
                upper = lane >= jnp.full((C, B), first + q, BF16)
                up = [table_i[DMAX + q + m * rate_r] for m in (-1, 0, 1)]
                low = [table_j[DMAX + q + m * rate_c] for m in (-1, 0, 1)]
                taps = [
                    jnp.where(upper, up[u] + up_window[v], low[v] + low_window[u])
                    for u in range(3)
                    for v in range(3)
                ]
                parts.append(jnp.concatenate([jnp.maximum(x, zero) for x in taps], 0))
            full = dot(short, jnp.concatenate(parts, 1), NN)
            store_rows(full, bias, 0, stage32.at[chunk], 16)
            round_rows(stage32.at[chunk], stage.at[chunk], 16)
            here = pair_hbm.at[:, pl.ds(first + chunk * 16, 16), :]
            saves.append(pltpu.make_async_copy(stage.at[chunk], here, sems.at[1 + chunk]))
            saves[-1].start()
        for save in saves:
            save.wait()


def shape(dims, kind):
    return jax.ShapeDtypeStruct(dims, kind)


SMEM = pl.BlockSpec(memory_space=pltpu.SMEM)
VMEM = pl.BlockSpec(memory_space=pltpu.VMEM)
ANY = pl.BlockSpec(memory_space=pl.ANY)
HBM = pl.BlockSpec(memory_space=pltpu.HBM)


def call(kernel, in_specs, out_shape, out_specs, scratch=(), aliases={}):
    return pl.pallas_call(
        kernel,
        out_shape=out_shape,
        in_specs=in_specs,
        out_specs=out_specs,
        scratch_shapes=list(scratch),
        input_output_aliases=aliases,
        compiler_params=pltpu.CompilerParams(vmem_limit_bytes=VMEM_BYTES),
    )


def gradients(fold_map, dilation, pieces, conv_weight, conv_bias, cot, cot_cols):
    return call(
        gradient_kernel,
        [SMEM, SMEM] + [VMEM] * 6 + [HBM] * 3,
        (shape((12, C, B), F32), shape((12, C, B), F32), shape((6, C, B), F32), shape((C, B, B), BF16)),
        (VMEM, VMEM, VMEM, HBM),
        [
            pltpu.VMEM((18, C, B), F32),
            pltpu.VMEM((4, B, NK), F32),
            pltpu.VMEM((4, B, NK), BF16),
            pltpu.VMEM((4, NK // B, 8 * B, B), F32),
            pltpu.VMEM((18, C, B), F32),
            pltpu.VMEM((C, NK), F32),
            pltpu.VMEM((B + 2 * DMAX, C, B), BF16),
            pltpu.VMEM((C, B, B), BF16),
            pltpu.VMEM((B, C, B), BF16),
            pltpu.VMEM((B, C, B), BF16),
            pltpu.VMEM((C * (B + PAD), B), F32),
            pltpu.VMEM((C * (B + PAD), B), F32),
            pltpu.VMEM((C, B, B), BF16),
            pltpu.VMEM((1, C), F32),
            pltpu.SemaphoreType.DMA((4,)),
        ],
    )(fold_map, dilation, *pieces, conv_weight, repeat_table(), conv_bias, cot, cot_cols)


def fold(which, fold_map, dilation, around, conv_weight, conv_bias, pair, after):
    first, count = PIECES[which]
    return call(
        functools.partial(fold_kernel, first, count),
        [SMEM, SMEM, VMEM, VMEM, HBM, HBM, ANY],
        (shape((C, B, B), BF16), shape((8, B), F32)),
        (HBM, VMEM),
        [
            pltpu.VMEM((count + 2 * DMAX, C, B), BF16),
            pltpu.VMEM((count + 2 * DMAX, C, B), BF16),
            pltpu.VMEM((count // 16, C * (16 + PAD), B), F32),
            pltpu.VMEM((count // 16, C, 16, B), BF16),
            pltpu.VMEM((1, C), F32),
            pltpu.SemaphoreType.DMA((1 + count // 16,)),
        ],
        {5: 0},
    )(fold_map, dilation, around, conv_weight, conv_bias, pair, after)


def after_core_kernel(keep, got, own, to1, to2, to3):
    z = place_of()[0]
    total = [(keep[k] + got[k]).astype(BF16) for k in range(8, 12)]
    for step, out in ((0, own), (1, to1), (2, to2), (3, to3)):
        first = (z ^ step) * 2
        for k in range(2):
            out[k] = (keep[first + k] + got[first + k]).astype(BF16)
        for k in range(4):
            out[2 + k] = total[k]


def sum4(own, a, b, c, k):
    return (own[k].astype(F32) + a[k].astype(F32)) + (b[k].astype(F32) + c[k].astype(F32))


def after_z_kernel(keep, a, b, c, token, own, other):
    x = place_of()[1]
    own[0] = sum4(keep, a, b, c, x).astype(BF16)
    other[0] = sum4(keep, a, b, c, 1 - x).astype(BF16)
    for k in range(4):
        total = sum4(keep, a, b, c, 2 + k).astype(BF16)
        own[1 + k] = total
        other[1 + k] = total


def after_x_kernel(keep, a, b, c, token, own):
    for k in range(5):
        own[k] = sum4(keep, a, b, c, k).astype(BF16)


def after_y_kernel(keep, a, b, c, grad_embed, grad_weight, grad_bias):
    grad_embed[...] = sum4(keep, a, b, c, 0) * (2048.0**-0.5)
    total = jnp.concatenate([sum4(keep, a, b, c, 1 + k) for k in range(4)], 1) * (1.0 / 2048.0)
    turned = total.T
    grad_weight[...] = turned[:432].reshape(9, C, C)
    grad_bias[...] = turned[432:433]


def body(bin_embed, conv_weight, conv_bias, dilation, fold_map, cotangent):
    fold_map = fold_map.T

    def swap(value, fold_bits, col_bits):
        route = [
            (f * 16 + c, (f ^ fold_bits) * 16 + (c ^ col_bits)) for f in range(8) for c in range(16)
        ]
        return lax.ppermute(value, ("fold", "col"), route)

    core, xlo, both = swap(bin_embed, 0, 1), swap(bin_embed, 0, 2), swap(bin_embed, 0, 3)
    quad = call(quad_kernel, [VMEM] * 4, shape((4, C, B), BF16), VMEM)(bin_embed, core, xlo, both)
    z1, z2, z3 = (swap(quad, 0, 4 * step) for step in (1, 2, 3))
    pieces = (quad, z1, z2, z3)

    cot = cotangent[0, 0]
    cot_cols = jnp.transpose(cot, (2, 0, 1))
    weight, bias = conv_weight.reshape(9 * C, C), conv_bias.reshape(1, C)
    send, keep, around, pair_out = gradients(
        fold_map, dilation, pieces, weight, bias, cot, cot_cols
    )

    def next_rows(which, pair_out, after):
        return fold(which, fold_map, dilation, around, weight, bias, pair_out, after)

    got = swap(send, 0, 1)
    half, part = shape((6, C, B), BF16), shape((5, C, B), BF16)
    keep, to1, to2, to3 = call(
        after_core_kernel, [VMEM, VMEM], (half,) * 4, (VMEM,) * 4
    )(keep, got)
    pair_out, token = next_rows(0, pair_out, keep)
    a, b, c = swap(to1, 0, 4), swap(to2, 0, 8), swap(to3, 0, 12)
    keep, other = call(
        after_z_kernel, [VMEM] * 4 + [ANY], (part, part), (VMEM, VMEM)
    )(keep, a, b, c, token)
    pair_out, token = next_rows(1, pair_out, keep)
    a, b, c = swap(other, 0, 2), swap(keep, 1, 0), swap(other, 1, 2)
    keep = call(after_x_kernel, [VMEM] * 4 + [ANY], part, VMEM)(keep, a, b, c, token)
    pair_out, token = next_rows(2, pair_out, keep)
    a, b, c = swap(keep, 2, 0), swap(keep, 4, 0), swap(keep, 6, 0)
    grad_embed, grad_weight, grad_bias = call(
        after_y_kernel,
        [VMEM] * 4,
        (shape((C, B), F32), shape((9, C, C), F32), shape((1, C), F32)),
        (VMEM,) * 3,
    )(keep, a, b, c)
    return pair_out[None, None], grad_embed, grad_weight, grad_bias.reshape(C)


def solution(mesh):
    placed = (P(None, "col"), P(), P(), P(), P(), P("fold", "col", None, None, None))
    return jax.shard_map(
        body,
        mesh=mesh,
        in_specs=placed,
        out_specs=(P("fold", "col", None, None, None), P(None, "col"), P(), P()),
        check_vma=False,
    )
```

```python
import functools

import jax
import jax.numpy as jnp
import numpy as np
from jax import lax
from jax.experimental import pallas as pl
from jax.experimental.pallas import tpu as pltpu
from jax.sharding import PartitionSpec as P

C = 48
B = 128
DMAX = 16
NK = 512
OUTSIDE = -16384.0
F32 = jnp.float32
BF16 = jnp.bfloat16
UNROLL = 16
PARTS = 4
ROWS = 32
PAD = 8
PIECES = ((0, 48), (48, 48), (96, 32))
VMEM_BYTES = 36 * 1024 * 1024

NT = (((1,), (1,)), ((), ()))
TN = (((0,), (0,)), ((), ()))
NN = (((1,), (0,)), ((), ()))


def dot(a, b, dims):
    return lax.dot_general(a, b, dims, preferred_element_type=F32)


def repeat_table():
    table = np.zeros((2, 144, NK), np.float32)
    for u in range(3):
        for v in range(3):
            for i in range(C):
                column = (3 * u + v) * C + i
                table[0, u * C + i, column] = 1.0
                table[1, v * C + i, column] = 1.0
    return jnp.asarray(table, BF16)


def position():
    return lax.axis_index("fold"), lax.axis_index("col")


def place_of():
    col = position()[1]
    return col // 4, (col // 2) % 2, col % 2


def prepare_kernel(
    fold_map, dilation, own, conv_weight, conv_bias, cot,
    meta, own_here, wide, short, bias, rows,
    cot32,
):
    fold, col = position()
    slot = fold * 16 + col
    for k in range(2):
        meta[k] = fold_map[k, slot]
        meta[2 + k] = dilation[k]
    own_here[...] = own[...]
    weight = conv_weight[...].astype(F32).T
    wide[...] = jnp.concatenate([weight, jnp.zeros((C, NK - 432), F32)], 1)
    short[...] = weight.astype(BF16)
    bias[...] = jnp.broadcast_to(conv_bias[...], (B, C)).T
    for c in range(C):
        cot32[c * (B + PAD) : c * (B + PAD) + B, :] = cot[c].astype(F32)
    for q in range(B):
        rows[q] = cot32[pl.ds(q, C, stride=B + PAD), :].astype(BF16)


def quad_kernel(own, core, xlo, both, out):
    for k, block in enumerate((own, core, xlo, both)):
        out[k] = block[...]


def fill_blocks(quad, z1, z2, z3, blocks):
    z, x, c = place_of()
    blocks[0] = jnp.full((C, B), OUTSIDE, F32)
    blocks[17] = jnp.full((C, B), OUTSIDE, F32)
    for step, got in ((0, quad), (1, z1), (2, z2), (3, z3)):
        there = 1 + (z ^ step) * 4
        for k in range(4):
            blocks[there + (x ^ (k // 2)) * 2 + (c ^ (k % 2))] = got[k].astype(F32)


def spread_lanes(blocks, tile, table, first, count):
    before, here, after = blocks[tile], blocks[tile + 1], blocks[tile + 2]
    for q in range(first - DMAX, first + count + DMAX):
        source, lane = (before, q + B) if q < 0 else ((here, q) if q < B else (after, q - B))
        table[q - first + DMAX] = jnp.broadcast_to(source[:, lane : lane + 1], (C, B)).astype(BF16)


def windows(blocks, tile, rate):
    lane = lax.broadcasted_iota(jnp.int32, (C, B), 1)
    before, here, after = blocks[tile], blocks[tile + 1], blocks[tile + 2]
    low = jnp.where(lane < rate, pltpu.roll(before, rate, 1), pltpu.roll(here, rate, 1))
    high = jnp.where(lane >= B - rate, pltpu.roll(after, B - rate, 1), pltpu.roll(here, B - rate, 1))
    return [low.astype(BF16), here.astype(BF16), high.astype(BF16)]


def scatter_back(grads, tile, rate, shifted):
    lane = lax.broadcasted_iota(jnp.int32, (C, B), 1)
    low, here, high = shifted
    low = pltpu.roll(low, B - rate, 1)
    high = pltpu.roll(high, rate, 1)
    zero = jnp.zeros((C, B), F32)
    grads[tile] += jnp.where(lane >= B - rate, low, zero)
    grads[tile + 2] += jnp.where(lane < rate, high, zero)
    grads[tile + 1] += (
        jnp.where(lane < B - rate, low, zero) + here + jnp.where(lane >= rate, high, zero)
    )


def store_rows(full, bias, first, stage32, count):
    for k in range(full.shape[1] // B):
        stage32[pl.ds(first + k, C, stride=count + PAD), :] = full[:, k * B : (k + 1) * B] + bias


def round_rows(stage32, stage, count):
    for c in range(C):
        stage[c] = stage32[c * (count + PAD) : c * (count + PAD) + count, :].astype(BF16)


def gradient_kernel(
    meta, quad, z1, z2, z3, wide, short, bias, repeat, rows, cols_hbm,
    send, keep, around, pair_hbm,
    blocks, shift, minus, sums, grads, wgrad, table, cols, stage32, stage, sems,
):
    tile_i, tile_j, rate_r, rate_c = meta[0], meta[1], meta[2], meta[3]
    core_index = place_of()[2]
    load_cols = pltpu.make_async_copy(cols_hbm, cols, sems.at[0])
    load_cols.start()
    fill_blocks(quad, z1, z2, z3, blocks)
    for k in range(3):
        around[k] = blocks[tile_i + k]
        around[3 + k] = blocks[tile_j + k]
    one, zero = jnp.ones((), BF16), jnp.zeros((), BF16)
    column = lax.broadcasted_iota(jnp.int32, (B, NK), 1)
    bias_mark = jnp.where(column == 432, 1.0, 0.0)
    grads[...] = jnp.zeros_like(grads)
    weight_wide = wide[...]
    empty = jnp.zeros((C, NK), F32)

    def tables(slot, tile, rate, which, mark):
        table = dot(jnp.concatenate(windows(blocks, tile, rate), 0), repeat[which], TN)
        minus[slot] = (-table).astype(BF16)
        shift[slot] = table + bias_mark if mark else table

    def back_sums(slot, tile, rate, which):
        tiles = []
        for at in range(NK // B):
            total = sums[slot, at, pl.ds(0, B, stride=8), :]
            for part in range(1, 8):
                total += sums[slot, at, pl.ds(part, B, stride=8), :]
            tiles.append(total)
        total = jnp.concatenate(tiles, 1)
        high = total.astype(BF16)
        low = (total - high.astype(F32)).astype(BF16)
        merged = dot(repeat[which], high, NT) + dot(repeat[which], low, NT)
        scatter_back(grads, tile, rate, [merged[k * C : (k + 1) * C] for k in range(3)])

    def loop(steps, start, first=0, last=B):
        def several(outer, carry):
            for inner in range(UNROLL):
                for step in steps:
                    carry = step(outer * UNROLL + inner, carry)
            return carry

        return lax.fori_loop(first // UNROLL, last // UNROLL, several, start)

    def take(slot, q, products, total):
        weighted = products * weight_wide
        partial = weighted[:8]
        for part in range(1, C // 8):
            partial += weighted[8 * part : 8 * part + 8]
        for at in range(NK // B):
            sums[slot, at, pl.ds(pl.multiple_of(q * 8, 8), 8), :] = partial[:, at * B : (at + 1) * B]
        return total + products * shift[slot, pl.ds(q, 1), :]

    def row_of(q):
        return rows[q]

    def col_of(q):
        return cols[q]

    @pl.when(tile_i < tile_j)
    def one_tile():
        spread_lanes(blocks, tile_i, table, 0, B)
        bias_now, short_now = bias[...], short[...]
        window = windows(blocks, tile_j, rate_c)

        def some(step, carry):
            parts = []
            for k in range(ROWS):
                at = [table[DMAX + step * ROWS + k + m * rate_r] for m in (-1, 0, 1)]
                taps = [jnp.maximum(at[u] + window[v], zero) for u in range(3) for v in range(3)]
                parts.append(jnp.concatenate(taps, 0))
            store_rows(dot(short_now, jnp.concatenate(parts, 1), NN), bias_now, step * ROWS, stage32, B)
            return carry

        lax.fori_loop(0, B // ROWS, some, 0)
        round_rows(stage32, stage, B)
        save_pair = pltpu.make_async_copy(stage, pair_hbm, sems.at[1])
        save_pair.start()

        tables(0, tile_i, rate_r, 0, True)
        tables(1, tile_j, rate_c, 1, False)
        load_cols.wait()

        def half(slot, other, grad_of):
            def step(q, total):
                at = jnp.broadcast_to(shift[slot, pl.ds(q, 1), :], (16, NK)).astype(BF16)
                at = jnp.concatenate([at] * (B // 16), 0)
                mask = jnp.where(at > minus[other], one, zero)
                return take(slot, q, dot(grad_of(q), mask, NN), total)

            return step

        wgrad[...] = loop([half(0, 1, row_of), half(1, 0, col_of)], empty)
        back_sums(0, tile_i, rate_r, 0)
        back_sums(1, tile_j, rate_c, 1)
        save_pair.wait()

    @pl.when(tile_i > tile_j)
    def two_triangles():
        tables(0, tile_i, rate_r, 0, True)
        tables(1, tile_i, rate_c, 1, False)
        tables(2, tile_j, rate_c, 1, True)
        tables(3, tile_j, rate_r, 0, False)
        load_cols.wait()
        lane = lax.broadcasted_iota(jnp.int32, (C, B), 1).astype(BF16)

        def half(slot, other, grad_of, side, live):
            def step(q, total):
                at = jnp.broadcast_to(shift[slot, pl.ds(q, 1), :], (16, NK)).astype(BF16)
                at = jnp.concatenate([at] * ((live.stop - live.start) // 16), 0)
                mask = jnp.where(at > minus[other, live, :], one, zero)
                pads = [jnp.zeros((n, NK), BF16) for n in (live.start, B - live.stop)]
                mask = jnp.concatenate([x for x in (pads[0], mask, pads[1]) if x.shape[0]], 0)
                place = jnp.full((C, B), q, F32).astype(BF16)
                grad = jnp.where(side(lane, place), grad_of(q), zero)
                return take(slot, q, dot(grad, mask, NN), total)

            return step

        total = empty
        for part in range(PARTS):
            lines = (part * B // PARTS, (part + 1) * B // PARTS)
            after, before = slice(lines[0], B), slice(0, lines[1])
            total = loop(
                [
                    half(0, 1, row_of, lambda s, r: s >= r, after),
                    half(1, 0, col_of, lambda r, s: r <= s, before),
                    half(2, 3, row_of, lambda s, r: s < r, before),
                    half(3, 2, col_of, lambda r, s: r > s, after),
                ],
                total,
                *lines,
            )
        wgrad[...] = total
        back_sums(0, tile_i, rate_r, 0)
        back_sums(1, tile_i, rate_c, 1)
        back_sums(2, tile_j, rate_c, 1)
        back_sums(3, tile_j, rate_r, 0)

    for pair in range(8):
        send[pair] = grads[1 + 2 * pair + (1 - core_index)]
        keep[pair] = grads[1 + 2 * pair + core_index]
    total = wgrad[...]
    for part in range(4):
        piece = total[:, part * B : (part + 1) * B]
        send[8 + part] = piece
        keep[8 + part] = piece


def fold_kernel(
    first, count, meta, around, short, bias, pair_before, after,
    pair_hbm, token,
    table_i, table_j, stage32, stage, sems,
):
    tile_i, tile_j, rate_r, rate_c = meta[0], meta[1], meta[2], meta[3]
    token[...] = jnp.zeros_like(token)

    @pl.when(tile_i > tile_j)
    def two_triangles():
        spread_lanes(around, 0, table_i, first, count)
        spread_lanes(around, 3, table_j, first, count)
        up_window, low_window = windows(around, 0, rate_c), windows(around, 3, rate_r)
        lane = lax.broadcasted_iota(jnp.int32, (C, B), 1).astype(BF16)
        short_now, bias_now, zero = short[...], bias[...], jnp.zeros((), BF16)
        saves = []
        for chunk in range(count // 16):
            parts = []
            for k in range(16):
                q = chunk * 16 + k
                upper = lane >= jnp.full((C, B), first + q, BF16)
                up = [table_i[DMAX + q + m * rate_r] for m in (-1, 0, 1)]
                low = [table_j[DMAX + q + m * rate_c] for m in (-1, 0, 1)]
                taps = [
                    jnp.where(upper, up[u] + up_window[v], low[v] + low_window[u])
                    for u in range(3)
                    for v in range(3)
                ]
                parts.append(jnp.concatenate([jnp.maximum(x, zero) for x in taps], 0))
            full = dot(short_now, jnp.concatenate(parts, 1), NN)
            store_rows(full, bias_now, 0, stage32.at[chunk], 16)
            round_rows(stage32.at[chunk], stage.at[chunk], 16)
            here = pair_hbm.at[:, pl.ds(first + chunk * 16, 16), :]
            saves.append(pltpu.make_async_copy(stage.at[chunk], here, sems.at[chunk]))
            saves[-1].start()
        for save in saves:
            save.wait()


def shape(dims, kind):
    return jax.ShapeDtypeStruct(dims, kind)


SMEM = pl.BlockSpec(memory_space=pltpu.SMEM)
VMEM = pl.BlockSpec(memory_space=pltpu.VMEM)
ANY = pl.BlockSpec(memory_space=pl.ANY)
HBM = pl.BlockSpec(memory_space=pltpu.HBM)


def call(kernel, in_specs, out_shape, out_specs, scratch=(), aliases={}):
    return pl.pallas_call(
        kernel,
        out_shape=out_shape,
        in_specs=in_specs,
        out_specs=out_specs,
        scratch_shapes=list(scratch),
        input_output_aliases=aliases,
        compiler_params=pltpu.CompilerParams(vmem_limit_bytes=VMEM_BYTES),
    )


def prepare(fold_map, dilation, own, conv_weight, conv_bias, cot):
    return call(
        prepare_kernel,
        [SMEM, SMEM] + [VMEM] * 4,
        (
            shape((4,), jnp.int32),
            shape((C, B), BF16),
            shape((C, NK), F32),
            shape((C, 432), BF16),
            shape((C, B), F32),
            shape((B, C, B), BF16),
        ),
        (SMEM,) + (VMEM,) * 5,
        [pltpu.VMEM((C * (B + PAD), B), F32)],
    )(fold_map, dilation, own, conv_weight, conv_bias, cot)


def gradients(meta, pieces, wide, short, bias, rows, cols):
    return call(
        gradient_kernel,
        [SMEM] + [VMEM] * 9 + [HBM],
        (shape((12, C, B), F32), shape((12, C, B), F32), shape((6, C, B), F32), shape((C, B, B), BF16)),
        (VMEM, VMEM, VMEM, HBM),
        [
            pltpu.VMEM((18, C, B), F32),
            pltpu.VMEM((4, B, NK), F32),
            pltpu.VMEM((4, B, NK), BF16),
            pltpu.VMEM((4, NK // B, 8 * B, B), F32),
            pltpu.VMEM((18, C, B), F32),
            pltpu.VMEM((C, NK), F32),
            pltpu.VMEM((B + 2 * DMAX, C, B), BF16),
            pltpu.VMEM((B, C, B), BF16),
            pltpu.VMEM((C * (B + PAD), B), F32),
            pltpu.VMEM((C, B, B), BF16),
            pltpu.SemaphoreType.DMA((2,)),
        ],
    )(meta, *pieces, wide, short, bias, repeat_table(), rows, cols)


def fold(which, meta, around, short, bias, pair, after):
    first, count = PIECES[which]
    return call(
        functools.partial(fold_kernel, first, count),
        [SMEM, VMEM, VMEM, VMEM, HBM, ANY],
        (shape((C, B, B), BF16), shape((8, B), F32)),
        (HBM, VMEM),
        [
            pltpu.VMEM((count + 2 * DMAX, C, B), BF16),
            pltpu.VMEM((count + 2 * DMAX, C, B), BF16),
            pltpu.VMEM((count // 16, C * (16 + PAD), B), F32),
            pltpu.VMEM((count // 16, C, 16, B), BF16),
            pltpu.SemaphoreType.DMA((count // 16,)),
        ],
        {4: 0},
    )(meta, around, short, bias, pair, after)


def after_core_kernel(keep, got, own, to1, to2, to3):
    z = place_of()[0]
    total = [(keep[k] + got[k]).astype(BF16) for k in range(8, 12)]
    for step, out in ((0, own), (1, to1), (2, to2), (3, to3)):
        first = (z ^ step) * 2
        for k in range(2):
            out[k] = (keep[first + k] + got[first + k]).astype(BF16)
        for k in range(4):
            out[2 + k] = total[k]


def sum4(own, a, b, c, k):
    return (own[k].astype(F32) + a[k].astype(F32)) + (b[k].astype(F32) + c[k].astype(F32))


def after_z_kernel(keep, a, b, c, token, own, other):
    x = place_of()[1]
    own[0] = sum4(keep, a, b, c, x).astype(BF16)
    other[0] = sum4(keep, a, b, c, 1 - x).astype(BF16)
    for k in range(4):
        total = sum4(keep, a, b, c, 2 + k).astype(BF16)
        own[1 + k] = total
        other[1 + k] = total


def after_x_kernel(keep, a, b, c, token, own):
    for k in range(5):
        own[k] = sum4(keep, a, b, c, k).astype(BF16)


def after_y_kernel(keep, a, b, c, grad_embed, grad_weight, grad_bias):
    grad_embed[...] = sum4(keep, a, b, c, 0) * (2048.0**-0.5)
    total = jnp.concatenate([sum4(keep, a, b, c, 1 + k) for k in range(4)], 1) * (1.0 / 2048.0)
    turned = total.T
    grad_weight[...] = turned[:432].reshape(9, C, C)
    grad_bias[...] = turned[432:433]


def body(bin_embed, conv_weight, conv_bias, dilation, fold_map, cotangent):
    fold_map = fold_map.T

    def swap(value, fold_bits, col_bits):
        route = [
            (f * 16 + c, (f ^ fold_bits) * 16 + (c ^ col_bits)) for f in range(8) for c in range(16)
        ]
        return lax.ppermute(value, ("fold", "col"), route)

    core, xlo, both = swap(bin_embed, 0, 1), swap(bin_embed, 0, 2), swap(bin_embed, 0, 3)
    cot = cotangent[0, 0]
    weight, bias = conv_weight.reshape(9 * C, C), conv_bias.reshape(1, C)
    meta, own, wide, short, bias, rows = prepare(fold_map, dilation, bin_embed, weight, bias, cot)
    quad = call(quad_kernel, [VMEM] * 4, shape((4, C, B), BF16), VMEM)(own, core, xlo, both)
    z1, z2, z3 = (swap(quad, 0, 4 * step) for step in (1, 2, 3))
    cols = jnp.transpose(cot, (2, 0, 1))
    send, keep, around, pair_out = gradients(meta, (quad, z1, z2, z3), wide, short, bias, rows, cols)

    def next_rows(which, pair_out, after):
        return fold(which, meta, around, short, bias, pair_out, after)

    got = swap(send, 0, 1)
    half, part = shape((6, C, B), BF16), shape((5, C, B), BF16)
    keep, to1, to2, to3 = call(
        after_core_kernel, [VMEM, VMEM], (half,) * 4, (VMEM,) * 4
    )(keep, got)
    pair_out, token = next_rows(0, pair_out, keep)
    a, b, c = swap(to1, 0, 4), swap(to2, 0, 8), swap(to3, 0, 12)
    keep, other = call(
        after_z_kernel, [VMEM] * 4 + [ANY], (part, part), (VMEM, VMEM)
    )(keep, a, b, c, token)
    pair_out, token = next_rows(1, pair_out, keep)
    a, b, c = swap(other, 0, 2), swap(keep, 1, 0), swap(other, 1, 2)
    keep = call(after_x_kernel, [VMEM] * 4 + [ANY], part, VMEM)(keep, a, b, c, token)
    pair_out, token = next_rows(2, pair_out, keep)
    a, b, c = swap(keep, 2, 0), swap(keep, 4, 0), swap(keep, 6, 0)
    grad_embed, grad_weight, grad_bias = call(
        after_y_kernel,
        [VMEM] * 4,
        (shape((C, B), F32), shape((9, C, C), F32), shape((1, C), F32)),
        (VMEM,) * 3,
    )(keep, a, b, c)
    return pair_out[None, None], grad_embed, grad_weight, grad_bias.reshape(C)


def solution(mesh):
    placed = (P(None, "col"), P(), P(), P(), P(), P("fold", "col", None, None, None))
    return jax.shard_map(
        body,
        mesh=mesh,
        in_specs=placed,
        out_specs=(P("fold", "col", None, None, None), P(None, "col"), P(), P()),
        check_vma=False,
    )
```

```python
import functools

import jax
import jax.numpy as jnp
import numpy as np
from jax import lax
from jax.experimental import pallas as pl
from jax.experimental.pallas import tpu as pltpu
from jax.sharding import PartitionSpec as P

C = 48
B = 128
DMAX = 16
NK = 512
OUTSIDE = -16384.0
F32 = jnp.float32
BF16 = jnp.bfloat16
UNROLL = 16
PARTS = 4
ROWS = 32
PAD = 8
PIECES = ((0, 48), (48, 48), (96, 32))
VMEM_BYTES = 40 * 1024 * 1024

NT = (((1,), (1,)), ((), ()))
TN = (((0,), (0,)), ((), ()))
NN = (((1,), (0,)), ((), ()))


def dot(a, b, dims):
    return lax.dot_general(a, b, dims, preferred_element_type=F32)


def repeat_table():
    table = np.zeros((2, 144, NK), np.float32)
    for u in range(3):
        for v in range(3):
            for i in range(C):
                column = (3 * u + v) * C + i
                table[0, u * C + i, column] = 1.0
                table[1, v * C + i, column] = 1.0
    return jnp.asarray(table, BF16)


def position():
    return lax.axis_index("fold"), lax.axis_index("col")


def tile_of(fold_map, dilation):
    fold, col = position()
    slot = fold * 16 + col
    return fold_map[0, slot], fold_map[1, slot], dilation[0, 0], dilation[1, 0]


def place_of():
    col = position()[1]
    return col // 4, (col // 2) % 2, col % 2


def quad_kernel(own, core, xlo, both, out):
    for k, block in enumerate((own, core, xlo, both)):
        out[k] = block[...]


def fill_blocks(quad, z1, z2, z3, blocks):
    z, x, c = place_of()
    blocks[0] = jnp.full((C, B), OUTSIDE, F32)
    blocks[17] = jnp.full((C, B), OUTSIDE, F32)
    for step, got in ((0, quad), (1, z1), (2, z2), (3, z3)):
        there = 1 + (z ^ step) * 4
        for k in range(4):
            blocks[there + (x ^ (k // 2)) * 2 + (c ^ (k % 2))] = got[k].astype(F32)


def spread_lanes(blocks, tile, table, first, count):
    before, here, after = blocks[tile], blocks[tile + 1], blocks[tile + 2]
    for q in range(first - DMAX, first + count + DMAX):
        source, lane = (before, q + B) if q < 0 else ((here, q) if q < B else (after, q - B))
        table[q - first + DMAX] = jnp.broadcast_to(source[:, lane : lane + 1], (C, B)).astype(BF16)


def windows(blocks, tile, rate):
    lane = lax.broadcasted_iota(jnp.int32, (C, B), 1)
    before, here, after = blocks[tile], blocks[tile + 1], blocks[tile + 2]
    low = jnp.where(lane < rate, pltpu.roll(before, rate, 1), pltpu.roll(here, rate, 1))
    high = jnp.where(lane >= B - rate, pltpu.roll(after, B - rate, 1), pltpu.roll(here, B - rate, 1))
    return [low.astype(BF16), here.astype(BF16), high.astype(BF16)]


def scatter_back(grads, tile, rate, shifted):
    lane = lax.broadcasted_iota(jnp.int32, (C, B), 1)
    low, here, high = shifted
    low = pltpu.roll(low, B - rate, 1)
    high = pltpu.roll(high, rate, 1)
    zero = jnp.zeros((C, B), F32)
    grads[tile] += jnp.where(lane >= B - rate, low, zero)
    grads[tile + 2] += jnp.where(lane < rate, high, zero)
    grads[tile + 1] += (
        jnp.where(lane < B - rate, low, zero) + here + jnp.where(lane >= rate, high, zero)
    )


def store_rows(full, bias, first, stage32, count):
    for k in range(full.shape[1] // B):
        stage32[pl.ds(first + k, C, stride=count + PAD), :] = full[:, k * B : (k + 1) * B] + bias


def round_rows(stage32, stage, count):
    for c in range(C):
        stage[c] = stage32[c * (count + PAD) : c * (count + PAD) + count, :].astype(BF16)


def gradient_kernel(
    fold_map, dilation, quad, z1, z2, z3, conv_weight, repeat, bias, cot, cols,
    send, keep, around, short, pair_hbm,
    blocks, shift, minus, sums, grads, wgrad, table, rows, cot32, stage32, stage, sem,
):
    tile_i, tile_j, rate_r, rate_c = tile_of(fold_map, dilation)
    core_index = place_of()[2]
    fill_blocks(quad, z1, z2, z3, blocks)
    for k in range(3):
        around[k] = blocks[tile_i + k]
        around[3 + k] = blocks[tile_j + k]
    one, zero = jnp.ones((), BF16), jnp.zeros((), BF16)
    column = lax.broadcasted_iota(jnp.int32, (B, NK), 1)
    bias_mark = jnp.where(column == 432, 1.0, 0.0)
    grads[...] = jnp.zeros_like(grads)
    weight = conv_weight[...].astype(F32).T
    short[...] = weight.astype(BF16)
    weight_wide = jnp.concatenate([weight, jnp.zeros((C, NK - 432), F32)], 1)
    empty = jnp.zeros((C, NK), F32)

    def tables(slot, tile, rate, which, mark):
        table = dot(jnp.concatenate(windows(blocks, tile, rate), 0), repeat[which], TN)
        minus[slot] = (-table).astype(BF16)
        shift[slot] = table + bias_mark if mark else table

    def back_sums(slot, tile, rate, which):
        tiles = []
        for at in range(NK // B):
            total = sums[slot, at, pl.ds(0, B, stride=8), :]
            for part in range(1, 8):
                total += sums[slot, at, pl.ds(part, B, stride=8), :]
            tiles.append(total)
        total = jnp.concatenate(tiles, 1)
        high = total.astype(BF16)
        low = (total - high.astype(F32)).astype(BF16)
        merged = dot(repeat[which], high, NT) + dot(repeat[which], low, NT)
        scatter_back(grads, tile, rate, [merged[k * C : (k + 1) * C] for k in range(3)])

    def loop(steps, start, first=0, last=B):
        def several(outer, carry):
            for inner in range(UNROLL):
                for step in steps:
                    carry = step(outer * UNROLL + inner, carry)
            return carry

        return lax.fori_loop(first // UNROLL, last // UNROLL, several, start)

    def take(slot, q, products, total):
        weighted = products * weight_wide
        partial = weighted[:8]
        for part in range(1, C // 8):
            partial += weighted[8 * part : 8 * part + 8]
        for at in range(NK // B):
            sums[slot, at, pl.ds(pl.multiple_of(q * 8, 8), 8), :] = partial[:, at * B : (at + 1) * B]
        return total + products * shift[slot, pl.ds(q, 1), :]

    def row_of(q):
        return rows[q]

    def col_of(q):
        return cols[q]

    def cotangent_here():
        for c in range(C):
            cot32[c * (B + PAD) : c * (B + PAD) + B, :] = cot[c].astype(F32)
        for q in range(B):
            rows[q] = cot32[pl.ds(q, C, stride=B + PAD), :].astype(BF16)

    @pl.when(tile_i < tile_j)
    def one_tile():
        spread_lanes(blocks, tile_i, table, 0, B)
        bias_now, short_now = bias[...], weight.astype(BF16)
        window = windows(blocks, tile_j, rate_c)

        def some(step, carry):
            parts = []
            for k in range(ROWS):
                at = [table[DMAX + step * ROWS + k + m * rate_r] for m in (-1, 0, 1)]
                taps = [jnp.maximum(at[u] + window[v], zero) for u in range(3) for v in range(3)]
                parts.append(jnp.concatenate(taps, 0))
            store_rows(dot(short_now, jnp.concatenate(parts, 1), NN), bias_now, step * ROWS, stage32, B)
            return carry

        lax.fori_loop(0, B // ROWS, some, 0)
        round_rows(stage32, stage, B)
        save_pair = pltpu.make_async_copy(stage, pair_hbm, sem)
        save_pair.start()

        tables(0, tile_i, rate_r, 0, True)
        tables(1, tile_j, rate_c, 1, False)
        cotangent_here()

        def half(slot, other, grad_of):
            def step(q, total):
                at = jnp.broadcast_to(shift[slot, pl.ds(q, 1), :], (16, NK)).astype(BF16)
                at = jnp.concatenate([at] * (B // 16), 0)
                mask = jnp.where(at > minus[other], one, zero)
                return take(slot, q, dot(grad_of(q), mask, NN), total)

            return step

        wgrad[...] = loop([half(0, 1, row_of), half(1, 0, col_of)], empty)
        back_sums(0, tile_i, rate_r, 0)
        back_sums(1, tile_j, rate_c, 1)
        save_pair.wait()

    @pl.when(tile_i > tile_j)
    def two_triangles():
        tables(0, tile_i, rate_r, 0, True)
        tables(1, tile_i, rate_c, 1, False)
        tables(2, tile_j, rate_c, 1, True)
        tables(3, tile_j, rate_r, 0, False)
        cotangent_here()
        lane = lax.broadcasted_iota(jnp.int32, (C, B), 1).astype(BF16)

        def half(slot, other, grad_of, side, live):
            def step(q, total):
                at = jnp.broadcast_to(shift[slot, pl.ds(q, 1), :], (16, NK)).astype(BF16)
                at = jnp.concatenate([at] * ((live.stop - live.start) // 16), 0)
                mask = jnp.where(at > minus[other, live, :], one, zero)
                pads = [jnp.zeros((n, NK), BF16) for n in (live.start, B - live.stop)]
                mask = jnp.concatenate([x for x in (pads[0], mask, pads[1]) if x.shape[0]], 0)
                place = jnp.full((C, B), q, F32).astype(BF16)
                grad = jnp.where(side(lane, place), grad_of(q), zero)
                return take(slot, q, dot(grad, mask, NN), total)

            return step

        total = empty
        for part in range(PARTS):
            lines = (part * B // PARTS, (part + 1) * B // PARTS)
            after, before = slice(lines[0], B), slice(0, lines[1])
            total = loop(
                [
                    half(0, 1, row_of, lambda s, r: s >= r, after),
                    half(1, 0, col_of, lambda r, s: r <= s, before),
                    half(2, 3, row_of, lambda s, r: s < r, before),
                    half(3, 2, col_of, lambda r, s: r > s, after),
                ],
                total,
                *lines,
            )
        wgrad[...] = total
        back_sums(0, tile_i, rate_r, 0)
        back_sums(1, tile_i, rate_c, 1)
        back_sums(2, tile_j, rate_c, 1)
        back_sums(3, tile_j, rate_r, 0)

    for pair in range(8):
        send[pair] = grads[1 + 2 * pair + (1 - core_index)]
        keep[pair] = grads[1 + 2 * pair + core_index]
    total = wgrad[...]
    for part in range(4):
        piece = total[:, part * B : (part + 1) * B]
        send[8 + part] = piece
        keep[8 + part] = piece


def fold_kernel(
    first, count, fold_map, dilation, around, short, bias, pair_before, after,
    pair_hbm, token,
    table_i, table_j, stage32, stage, sems,
):
    tile_i, tile_j, rate_r, rate_c = tile_of(fold_map, dilation)
    token[...] = jnp.zeros_like(token)

    @pl.when(tile_i > tile_j)
    def two_triangles():
        spread_lanes(around, 0, table_i, first, count)
        spread_lanes(around, 3, table_j, first, count)
        up_window, low_window = windows(around, 0, rate_c), windows(around, 3, rate_r)
        lane = lax.broadcasted_iota(jnp.int32, (C, B), 1).astype(BF16)
        short_now, bias_now, zero = short[...], bias[...], jnp.zeros((), BF16)
        saves = []
        for chunk in range(count // 16):
            parts = []
            for k in range(16):
                q = chunk * 16 + k
                upper = lane >= jnp.full((C, B), first + q, BF16)
                up = [table_i[DMAX + q + m * rate_r] for m in (-1, 0, 1)]
                low = [table_j[DMAX + q + m * rate_c] for m in (-1, 0, 1)]
                taps = [
                    jnp.where(upper, up[u] + up_window[v], low[v] + low_window[u])
                    for u in range(3)
                    for v in range(3)
                ]
                parts.append(jnp.concatenate([jnp.maximum(x, zero) for x in taps], 0))
            full = dot(short_now, jnp.concatenate(parts, 1), NN)
            store_rows(full, bias_now, 0, stage32.at[chunk], 16)
            round_rows(stage32.at[chunk], stage.at[chunk], 16)
            here = pair_hbm.at[:, pl.ds(first + chunk * 16, 16), :]
            saves.append(pltpu.make_async_copy(stage.at[chunk], here, sems.at[chunk]))
            saves[-1].start()
        for save in saves:
            save.wait()


def shape(dims, kind):
    return jax.ShapeDtypeStruct(dims, kind)


SMEM = pl.BlockSpec(memory_space=pltpu.SMEM)
VMEM = pl.BlockSpec(memory_space=pltpu.VMEM)
ANY = pl.BlockSpec(memory_space=pl.ANY)
HBM = pl.BlockSpec(memory_space=pltpu.HBM)


def call(kernel, in_specs, out_shape, out_specs, scratch=(), aliases={}):
    return pl.pallas_call(
        kernel,
        out_shape=out_shape,
        in_specs=in_specs,
        out_specs=out_specs,
        scratch_shapes=list(scratch),
        input_output_aliases=aliases,
        compiler_params=pltpu.CompilerParams(vmem_limit_bytes=VMEM_BYTES),
    )


def gradients(fold_map, dilation, pieces, conv_weight, conv_bias, cot, cot_cols):
    return call(
        gradient_kernel,
        [SMEM, SMEM] + [VMEM] * 9,
        (
            shape((12, C, B), F32),
            shape((12, C, B), F32),
            shape((6, C, B), F32),
            shape((C, 432), BF16),
            shape((C, B, B), BF16),
        ),
        (VMEM, VMEM, VMEM, VMEM, HBM),
        [
            pltpu.VMEM((18, C, B), F32),
            pltpu.VMEM((4, B, NK), F32),
            pltpu.VMEM((4, B, NK), BF16),
            pltpu.VMEM((4, NK // B, 8 * B, B), F32),
            pltpu.VMEM((18, C, B), F32),
            pltpu.VMEM((C, NK), F32),
            pltpu.VMEM((B + 2 * DMAX, C, B), BF16),
            pltpu.VMEM((B, C, B), BF16),
            pltpu.VMEM((C * (B + PAD), B), F32),
            pltpu.VMEM((C * (B + PAD), B), F32),
            pltpu.VMEM((C, B, B), BF16),
            pltpu.SemaphoreType.DMA,
        ],
    )(fold_map, dilation, *pieces, conv_weight, repeat_table(), conv_bias, cot, cot_cols)


def fold(which, fold_map, dilation, around, short, bias, pair, after):
    first, count = PIECES[which]
    return call(
        functools.partial(fold_kernel, first, count),
        [SMEM, SMEM, VMEM, VMEM, VMEM, HBM, ANY],
        (shape((C, B, B), BF16), shape((8, B), F32)),
        (HBM, VMEM),
        [
            pltpu.VMEM((count + 2 * DMAX, C, B), BF16),
            pltpu.VMEM((count + 2 * DMAX, C, B), BF16),
            pltpu.VMEM((count // 16, C * (16 + PAD), B), F32),
            pltpu.VMEM((count // 16, C, 16, B), BF16),
            pltpu.SemaphoreType.DMA((count // 16,)),
        ],
        {5: 0},
    )(fold_map, dilation, around, short, bias, pair, after)


def after_core_kernel(keep, got, own, to1, to2, to3):
    z = place_of()[0]
    total = [(keep[k] + got[k]).astype(BF16) for k in range(8, 12)]
    for step, out in ((0, own), (1, to1), (2, to2), (3, to3)):
        first = (z ^ step) * 2
        for k in range(2):
            out[k] = (keep[first + k] + got[first + k]).astype(BF16)
        for k in range(4):
            out[2 + k] = total[k]


def sum4(own, a, b, c, k):
    return (own[k].astype(F32) + a[k].astype(F32)) + (b[k].astype(F32) + c[k].astype(F32))


def after_z_kernel(keep, a, b, c, token, own, other):
    x = place_of()[1]
    own[0] = sum4(keep, a, b, c, x).astype(BF16)
    other[0] = sum4(keep, a, b, c, 1 - x).astype(BF16)
    for k in range(4):
        total = sum4(keep, a, b, c, 2 + k).astype(BF16)
        own[1 + k] = total
        other[1 + k] = total


def after_x_kernel(keep, a, b, c, token, own):
    for k in range(5):
        own[k] = sum4(keep, a, b, c, k).astype(BF16)


def after_y_kernel(keep, a, b, c, grad_embed, grad_weight, grad_bias):
    grad_embed[...] = sum4(keep, a, b, c, 0) * (2048.0**-0.5)
    total = jnp.concatenate([sum4(keep, a, b, c, 1 + k) for k in range(4)], 1) * (1.0 / 2048.0)
    turned = total.T
    grad_weight[...] = turned[:432].reshape(9, C, C)
    grad_bias[...] = turned[432:433]


def body(bin_embed, conv_weight, conv_bias, dilation, fold_map, cotangent):
    fold_map, dilation = fold_map.T, jnp.broadcast_to(dilation[:, None], (2, B))

    def swap(value, fold_bits, col_bits):
        route = [
            (f * 16 + c, (f ^ fold_bits) * 16 + (c ^ col_bits)) for f in range(8) for c in range(16)
        ]
        return lax.ppermute(value, ("fold", "col"), route)

    core, xlo, both = swap(bin_embed, 0, 1), swap(bin_embed, 0, 2), swap(bin_embed, 0, 3)
    quad = call(quad_kernel, [VMEM] * 4, shape((4, C, B), BF16), VMEM)(bin_embed, core, xlo, both)
    z1, z2, z3 = (swap(quad, 0, 4 * step) for step in (1, 2, 3))
    pieces = (quad, z1, z2, z3)

    cot = cotangent[0, 0]
    cot_cols = jnp.transpose(cot, (2, 0, 1))
    weight, bias = conv_weight.reshape(9 * C, C), jnp.broadcast_to(conv_bias[:, None], (C, B))
    send, keep, around, short, pair_out = gradients(
        fold_map, dilation, pieces, weight, bias, cot, cot_cols
    )

    def next_rows(which, pair_out, after):
        return fold(which, fold_map, dilation, around, short, bias, pair_out, after)

    got = swap(send, 0, 1)
    half, part = shape((6, C, B), BF16), shape((5, C, B), BF16)
    keep, to1, to2, to3 = call(
        after_core_kernel, [VMEM, VMEM], (half,) * 4, (VMEM,) * 4
    )(keep, got)
    pair_out, token = next_rows(0, pair_out, keep)
    a, b, c = swap(to1, 0, 4), swap(to2, 0, 8), swap(to3, 0, 12)
    keep, other = call(
        after_z_kernel, [VMEM] * 4 + [ANY], (part, part), (VMEM, VMEM)
    )(keep, a, b, c, token)
    pair_out, token = next_rows(1, pair_out, keep)
    a, b, c = swap(other, 0, 2), swap(keep, 1, 0), swap(other, 1, 2)
    keep = call(after_x_kernel, [VMEM] * 4 + [ANY], part, VMEM)(keep, a, b, c, token)
    pair_out, token = next_rows(2, pair_out, keep)
    a, b, c = swap(keep, 2, 0), swap(keep, 4, 0), swap(keep, 6, 0)
    grad_embed, grad_weight, grad_bias = call(
        after_y_kernel,
        [VMEM] * 4,
        (shape((C, B), F32), shape((9, C, C), F32), shape((1, C), F32)),
        (VMEM,) * 3,
    )(keep, a, b, c)
    return pair_out[None, None], grad_embed, grad_weight, grad_bias.reshape(C)


def solution(mesh):
    placed = (P(None, "col"), P(), P(), P(), P(), P("fold", "col", None, None, None))
    return jax.shard_map(
        body,
        mesh=mesh,
        in_specs=placed,
        out_specs=(P("fold", "col", None, None, None), P(None, "col"), P(), P()),
        check_vma=False,
    )
```

```python
import functools

import jax
import jax.numpy as jnp
import numpy as np
from jax import lax
from jax.experimental import pallas as pl
from jax.experimental.pallas import tpu as pltpu
from jax.sharding import PartitionSpec as P

C = 48
B = 128
DMAX = 16
NK = 512
OUTSIDE = -16384.0
F32 = jnp.float32
BF16 = jnp.bfloat16
UNROLL = 16
PARTS = 4
ROWS = 32
PAD = 8
PIECES = ((0, 48), (48, 48), (96, 32))
VMEM_BYTES = 40 * 1024 * 1024

NT = (((1,), (1,)), ((), ()))
TN = (((0,), (0,)), ((), ()))
NN = (((1,), (0,)), ((), ()))


def dot(a, b, dims):
    return lax.dot_general(a, b, dims, preferred_element_type=F32)


def repeat_table():
    table = np.zeros((2, 144, NK), np.float32)
    for u in range(3):
        for v in range(3):
            for i in range(C):
                column = (3 * u + v) * C + i
                table[0, u * C + i, column] = 1.0
                table[1, v * C + i, column] = 1.0
    return jnp.asarray(table, BF16)


def position():
    return lax.axis_index("fold"), lax.axis_index("col")


def tile_of(fold_map, dilation):
    fold, col = position()
    slot = fold * 16 + col
    return fold_map[0, slot], fold_map[1, slot], dilation[0, 0], dilation[1, 0]


def place_of():
    col = position()[1]
    return col // 4, (col // 2) % 2, col % 2


def quad_kernel(own, core, xlo, both, out):
    out[0] = own[0]
    for k, block in enumerate((core, xlo, both)):
        out[1 + k] = block[...]


def fill_blocks(quad, z1, z2, z3, blocks):
    z, x, c = place_of()
    blocks[0] = jnp.full((C, B), OUTSIDE, F32)
    blocks[17] = jnp.full((C, B), OUTSIDE, F32)
    for step, got in ((0, quad), (1, z1), (2, z2), (3, z3)):
        there = 1 + (z ^ step) * 4
        for k in range(4):
            blocks[there + (x ^ (k // 2)) * 2 + (c ^ (k % 2))] = got[k].astype(F32)


def spread_lanes(blocks, tile, table, first, count):
    before, here, after = blocks[tile], blocks[tile + 1], blocks[tile + 2]
    for q in range(first - DMAX, first + count + DMAX):
        source, lane = (before, q + B) if q < 0 else ((here, q) if q < B else (after, q - B))
        table[q - first + DMAX] = jnp.broadcast_to(source[:, lane : lane + 1], (C, B)).astype(BF16)


def windows(blocks, tile, rate):
    lane = lax.broadcasted_iota(jnp.int32, (C, B), 1)
    before, here, after = blocks[tile], blocks[tile + 1], blocks[tile + 2]
    low = jnp.where(lane < rate, pltpu.roll(before, rate, 1), pltpu.roll(here, rate, 1))
    high = jnp.where(lane >= B - rate, pltpu.roll(after, B - rate, 1), pltpu.roll(here, B - rate, 1))
    return [low.astype(BF16), here.astype(BF16), high.astype(BF16)]


def scatter_back(grads, tile, rate, shifted):
    lane = lax.broadcasted_iota(jnp.int32, (C, B), 1)
    low, here, high = shifted
    low = pltpu.roll(low, B - rate, 1)
    high = pltpu.roll(high, rate, 1)
    zero = jnp.zeros((C, B), F32)
    grads[tile] += jnp.where(lane >= B - rate, low, zero)
    grads[tile + 2] += jnp.where(lane < rate, high, zero)
    grads[tile + 1] += (
        jnp.where(lane < B - rate, low, zero) + here + jnp.where(lane >= rate, high, zero)
    )


def store_rows(full, bias, first, stage32, count):
    for k in range(full.shape[1] // B):
        stage32[pl.ds(first + k, C, stride=count + PAD), :] = full[:, k * B : (k + 1) * B] + bias


def round_rows(stage32, stage, count):
    for c in range(C):
        stage[c] = stage32[c * (count + PAD) : c * (count + PAD) + count, :].astype(BF16)


def gradient_kernel(
    fold_map, dilation, quad, z1, z2, z3, weight, repeat, bias, cot, cols,
    send, keep, around, meta, pair_hbm,
    blocks, shift, minus, sums, grads, wgrad, table, rows, cot32, stage32, stage, sem,
):
    tile_i, tile_j, rate_r, rate_c = tile_of(fold_map, dilation)
    core_index = place_of()[2]
    fill_blocks(quad, z1, z2, z3, blocks)
    for k in range(3):
        around[k] = blocks[tile_i + k]
        around[3 + k] = blocks[tile_j + k]
    one, zero = jnp.ones((), BF16), jnp.zeros((), BF16)
    column = lax.broadcasted_iota(jnp.int32, (B, NK), 1)
    bias_mark = jnp.where(column == 432, 1.0, 0.0)
    grads[...] = jnp.zeros_like(grads)
    for k, value in enumerate((tile_i, tile_j, rate_r, rate_c)):
        meta[k] = value
    weight_wide = jnp.concatenate([weight[...].astype(F32), jnp.zeros((C, NK - 432), F32)], 1)
    empty = jnp.zeros((C, NK), F32)

    def tables(slot, tile, rate, which, mark):
        table = dot(jnp.concatenate(windows(blocks, tile, rate), 0), repeat[which], TN)
        minus[slot] = (-table).astype(BF16)
        shift[slot] = table + bias_mark if mark else table

    def back_sums(slot, tile, rate, which):
        tiles = []
        for at in range(NK // B):
            total = sums[slot, at, pl.ds(0, B, stride=8), :]
            for part in range(1, 8):
                total += sums[slot, at, pl.ds(part, B, stride=8), :]
            tiles.append(total)
        total = jnp.concatenate(tiles, 1)
        high = total.astype(BF16)
        low = (total - high.astype(F32)).astype(BF16)
        merged = dot(repeat[which], high, NT) + dot(repeat[which], low, NT)
        scatter_back(grads, tile, rate, [merged[k * C : (k + 1) * C] for k in range(3)])

    def loop(steps, start, first=0, last=B):
        def several(outer, carry):
            for inner in range(UNROLL):
                for step in steps:
                    carry = step(outer * UNROLL + inner, carry)
            return carry

        return lax.fori_loop(first // UNROLL, last // UNROLL, several, start)

    def take(slot, q, products, total):
        weighted = products * weight_wide
        partial = weighted[:8]
        for part in range(1, C // 8):
            partial += weighted[8 * part : 8 * part + 8]
        for at in range(NK // B):
            sums[slot, at, pl.ds(pl.multiple_of(q * 8, 8), 8), :] = partial[:, at * B : (at + 1) * B]
        return total + products * shift[slot, pl.ds(q, 1), :]

    def row_of(q):
        return rows[q]

    def col_of(q):
        return cols[q]

    def cotangent_here():
        for c in range(C):
            cot32[c * (B + PAD) : c * (B + PAD) + B, :] = cot[c].astype(F32)
        for q in range(B):
            rows[q] = cot32[pl.ds(q, C, stride=B + PAD), :].astype(BF16)

    @pl.when(tile_i < tile_j)
    def one_tile():
        spread_lanes(blocks, tile_i, table, 0, B)
        bias_now, weight_now = bias[...], weight[...]
        window = windows(blocks, tile_j, rate_c)

        def some(step, carry):
            parts = []
            for k in range(ROWS):
                at = [table[DMAX + step * ROWS + k + m * rate_r] for m in (-1, 0, 1)]
                taps = [jnp.maximum(at[u] + window[v], zero) for u in range(3) for v in range(3)]
                parts.append(jnp.concatenate(taps, 0))
            store_rows(dot(weight_now, jnp.concatenate(parts, 1), NN), bias_now, step * ROWS, stage32, B)
            return carry

        lax.fori_loop(0, B // ROWS, some, 0)
        round_rows(stage32, stage, B)
        save_pair = pltpu.make_async_copy(stage, pair_hbm, sem)
        save_pair.start()

        tables(0, tile_i, rate_r, 0, True)
        tables(1, tile_j, rate_c, 1, False)
        cotangent_here()

        def half(slot, other, grad_of):
            def step(q, total):
                at = jnp.broadcast_to(shift[slot, pl.ds(q, 1), :], (16, NK)).astype(BF16)
                at = jnp.concatenate([at] * (B // 16), 0)
                mask = jnp.where(at > minus[other], one, zero)
                return take(slot, q, dot(grad_of(q), mask, NN), total)

            return step

        wgrad[...] = loop([half(0, 1, row_of), half(1, 0, col_of)], empty)
        back_sums(0, tile_i, rate_r, 0)
        back_sums(1, tile_j, rate_c, 1)
        save_pair.wait()

    @pl.when(tile_i > tile_j)
    def two_triangles():
        tables(0, tile_i, rate_r, 0, True)
        tables(1, tile_i, rate_c, 1, False)
        tables(2, tile_j, rate_c, 1, True)
        tables(3, tile_j, rate_r, 0, False)
        cotangent_here()
        lane = lax.broadcasted_iota(jnp.int32, (C, B), 1).astype(BF16)

        def half(slot, other, grad_of, side, live):
            def step(q, total):
                at = jnp.broadcast_to(shift[slot, pl.ds(q, 1), :], (16, NK)).astype(BF16)
                at = jnp.concatenate([at] * ((live.stop - live.start) // 16), 0)
                mask = jnp.where(at > minus[other, live, :], one, zero)
                pads = [jnp.zeros((n, NK), BF16) for n in (live.start, B - live.stop)]
                mask = jnp.concatenate([x for x in (pads[0], mask, pads[1]) if x.shape[0]], 0)
                place = jnp.full((C, B), q, F32).astype(BF16)
                grad = jnp.where(side(lane, place), grad_of(q), zero)
                return take(slot, q, dot(grad, mask, NN), total)

            return step

        total = empty
        for part in range(PARTS):
            lines = (part * B // PARTS, (part + 1) * B // PARTS)
            after, before = slice(lines[0], B), slice(0, lines[1])
            total = loop(
                [
                    half(0, 1, row_of, lambda s, r: s >= r, after),
                    half(1, 0, col_of, lambda r, s: r <= s, before),
                    half(2, 3, row_of, lambda s, r: s < r, before),
                    half(3, 2, col_of, lambda r, s: r > s, after),
                ],
                total,
                *lines,
            )
        wgrad[...] = total
        back_sums(0, tile_i, rate_r, 0)
        back_sums(1, tile_i, rate_c, 1)
        back_sums(2, tile_j, rate_c, 1)
        back_sums(3, tile_j, rate_r, 0)

    for pair in range(8):
        send[pair] = grads[1 + 2 * pair + (1 - core_index)]
        keep[pair] = grads[1 + 2 * pair + core_index]
    total = wgrad[...]
    for part in range(4):
        piece = total[:, part * B : (part + 1) * B]
        send[8 + part] = piece
        keep[8 + part] = piece


def fold_kernel(
    first, count, meta, around, weight, bias, pair_before, after, pair_hbm,
    table_i, table_j, stage32, stage, sems,
):
    tile_i, tile_j, rate_r, rate_c = meta[0], meta[1], meta[2], meta[3]

    @pl.when(tile_i > tile_j)
    def two_triangles():
        spread_lanes(around, 0, table_i, first, count)
        spread_lanes(around, 3, table_j, first, count)
        up_window, low_window = windows(around, 0, rate_c), windows(around, 3, rate_r)
        lane = lax.broadcasted_iota(jnp.int32, (C, B), 1).astype(BF16)
        weight_now, bias_now, zero = weight[...], bias[...], jnp.zeros((), BF16)
        saves = []
        for chunk in range(count // 16):
            parts = []
            for k in range(16):
                q = chunk * 16 + k
                upper = lane >= jnp.full((C, B), first + q, BF16)
                up = [table_i[DMAX + q + m * rate_r] for m in (-1, 0, 1)]
                low = [table_j[DMAX + q + m * rate_c] for m in (-1, 0, 1)]
                taps = [
                    jnp.where(upper, up[u] + up_window[v], low[v] + low_window[u])
                    for u in range(3)
                    for v in range(3)
                ]
                parts.append(jnp.concatenate([jnp.maximum(x, zero) for x in taps], 0))
            full = dot(weight_now, jnp.concatenate(parts, 1), NN)
            store_rows(full, bias_now, 0, stage32.at[chunk], 16)
            round_rows(stage32.at[chunk], stage.at[chunk], 16)
            here = pair_hbm.at[:, pl.ds(first + chunk * 16, 16), :]
            saves.append(pltpu.make_async_copy(stage.at[chunk], here, sems.at[chunk]))
            saves[-1].start()
        for save in saves:
            save.wait()


def shape(dims, kind):
    return jax.ShapeDtypeStruct(dims, kind)


SMEM = pl.BlockSpec(memory_space=pltpu.SMEM)
VMEM = pl.BlockSpec(memory_space=pltpu.VMEM)
ANY = pl.BlockSpec(memory_space=pl.ANY)
HBM = pl.BlockSpec(memory_space=pltpu.HBM)


def call(kernel, in_specs, out_shape, out_specs, scratch=(), aliases={}):
    return pl.pallas_call(
        kernel,
        out_shape=out_shape,
        in_specs=in_specs,
        out_specs=out_specs,
        scratch_shapes=list(scratch),
        input_output_aliases=aliases,
        compiler_params=pltpu.CompilerParams(vmem_limit_bytes=VMEM_BYTES),
    )


def gradients(fold_map, dilation, pieces, weight, bias, cot, cot_cols):
    return call(
        gradient_kernel,
        [SMEM, SMEM] + [VMEM] * 9,
        (
            shape((12, C, B), F32),
            shape((12, C, B), F32),
            shape((6, C, B), F32),
            shape((4,), jnp.int32),
            shape((C, B, B), BF16),
        ),
        (VMEM, VMEM, VMEM, SMEM, HBM),
        [
            pltpu.VMEM((18, C, B), F32),
            pltpu.VMEM((4, B, NK), F32),
            pltpu.VMEM((4, B, NK), BF16),
            pltpu.VMEM((4, NK // B, 8 * B, B), F32),
            pltpu.VMEM((18, C, B), F32),
            pltpu.VMEM((C, NK), F32),
            pltpu.VMEM((B + 2 * DMAX, C, B), BF16),
            pltpu.VMEM((B, C, B), BF16),
            pltpu.VMEM((C * (B + PAD), B), F32),
            pltpu.VMEM((C * (B + PAD), B), F32),
            pltpu.VMEM((C, B, B), BF16),
            pltpu.SemaphoreType.DMA,
        ],
    )(fold_map, dilation, *pieces, weight, repeat_table(), bias, cot, cot_cols)


def fold(which, meta, around, weight, bias, pair, after):
    first, count = PIECES[which]
    return call(
        functools.partial(fold_kernel, first, count),
        [SMEM, VMEM, VMEM, VMEM, HBM, ANY],
        shape((C, B, B), BF16),
        HBM,
        [
            pltpu.VMEM((count + 2 * DMAX, C, B), BF16),
            pltpu.VMEM((count + 2 * DMAX, C, B), BF16),
            pltpu.VMEM((count // 16, C * (16 + PAD), B), F32),
            pltpu.VMEM((count // 16, C, 16, B), BF16),
            pltpu.SemaphoreType.DMA((count // 16,)),
        ],
        {4: 0},
    )(meta, around, weight, bias, pair, after)


def after_core_kernel(keep, got, own, to1, to2, to3):
    z = place_of()[0]
    total = [(keep[k] + got[k]).astype(BF16) for k in range(8, 12)]
    for step, out in ((0, own), (1, to1), (2, to2), (3, to3)):
        first = (z ^ step) * 2
        for k in range(2):
            out[k] = (keep[first + k] + got[first + k]).astype(BF16)
        for k in range(4):
            out[2 + k] = total[k]


def sum4(own, a, b, c, k):
    return (own[k].astype(F32) + a[k].astype(F32)) + (b[k].astype(F32) + c[k].astype(F32))


def after_z_kernel(keep, a, b, c, pair, own, other):
    x = place_of()[1]
    own[0] = sum4(keep, a, b, c, x).astype(BF16)
    other[0] = sum4(keep, a, b, c, 1 - x).astype(BF16)
    for k in range(4):
        total = sum4(keep, a, b, c, 2 + k).astype(BF16)
        own[1 + k] = total
        other[1 + k] = total


def after_x_kernel(keep, a, b, c, pair, own):
    for k in range(5):
        own[k] = sum4(keep, a, b, c, k).astype(BF16)


def after_y_kernel(keep, a, b, c, grad_embed, grad_weight, grad_bias):
    grad_embed[...] = sum4(keep, a, b, c, 0) * (2048.0**-0.5)
    total = jnp.concatenate([sum4(keep, a, b, c, 1 + k) for k in range(4)], 1) * (1.0 / 2048.0)
    turned = total.T
    grad_weight[...] = turned[:432].reshape(9, C, C)
    grad_bias[...] = turned[432:433]


def body(bin_embed, conv_weight, conv_bias, dilation, fold_map, cotangent):
    fold_map, dilation = fold_map.T, jnp.broadcast_to(dilation[:, None], (2, B))

    def swap(value, fold_bits, col_bits):
        route = [
            (f * 16 + c, (f ^ fold_bits) * 16 + (c ^ col_bits)) for f in range(8) for c in range(16)
        ]
        return lax.ppermute(value, ("fold", "col"), route)

    core, xlo, both = swap(bin_embed, 0, 1), swap(bin_embed, 0, 2), swap(bin_embed, 0, 3)
    quad = call(quad_kernel, [VMEM] * 4, shape((4, C, B), BF16), VMEM)(
        jnp.broadcast_to(bin_embed[None], (2, C, B)), core, xlo, both
    )
    z1, z2, z3 = (swap(quad, 0, 4 * step) for step in (1, 2, 3))
    pieces = (quad, z1, z2, z3)

    cot = cotangent[0, 0]
    cot_cols = jnp.transpose(cot, (2, 0, 1))
    weight = jnp.transpose(conv_weight, (2, 0, 1)).reshape(C, 9 * C)
    bias = jnp.broadcast_to(conv_bias[:, None], (C, B))
    send, keep, around, meta, pair_out = gradients(
        fold_map, dilation, pieces, weight, bias, cot, cot_cols
    )

    def next_rows(which, pair_out, after):
        return fold(which, meta, around, weight, bias, pair_out, after)

    got = swap(send, 0, 1)
    half, part = shape((6, C, B), BF16), shape((5, C, B), BF16)
    keep, to1, to2, to3 = call(
        after_core_kernel, [VMEM, VMEM], (half,) * 4, (VMEM,) * 4
    )(keep, got)
    pair_out = next_rows(0, pair_out, keep)
    a, b, c = swap(to1, 0, 4), swap(to2, 0, 8), swap(to3, 0, 12)
    keep, other = call(
        after_z_kernel, [VMEM] * 4 + [HBM], (part, part), (VMEM, VMEM)
    )(keep, a, b, c, pair_out)
    pair_out = next_rows(1, pair_out, keep)
    a, b, c = swap(other, 0, 2), swap(keep, 1, 0), swap(other, 1, 2)
    keep = call(after_x_kernel, [VMEM] * 4 + [HBM], part, VMEM)(keep, a, b, c, pair_out)
    pair_out = next_rows(2, pair_out, keep)
    a, b, c = swap(keep, 2, 0), swap(keep, 4, 0), swap(keep, 6, 0)
    grad_embed, grad_weight, grad_bias = call(
        after_y_kernel,
        [VMEM] * 4,
        (shape((C, B), F32), shape((9, C, C), F32), shape((1, C), F32)),
        (VMEM,) * 3,
    )(keep, a, b, c)
    return pair_out[None, None], grad_embed, grad_weight, grad_bias.reshape(C)


def solution(mesh):
    placed = (P(None, "col"), P(), P(), P(), P(), P("fold", "col", None, None, None))
    return jax.shard_map(
        body,
        mesh=mesh,
        in_specs=placed,
        out_specs=(P("fold", "col", None, None, None), P(None, "col"), P(), P()),
        check_vma=False,
    )
```

```python
import functools

import jax
import jax.numpy as jnp
import numpy as np
from jax import lax
from jax.experimental import pallas as pl
from jax.experimental.pallas import tpu as pltpu
from jax.sharding import PartitionSpec as P

C = 48
B = 128
DMAX = 16
NK = 512
OUTSIDE = -16384.0
F32 = jnp.float32
BF16 = jnp.bfloat16
UNROLL = 16
PARTS = 4
ROWS = 32
PAD = 8
PIECES = ((0, 48), (48, 48), (96, 32))
VMEM_BYTES = 40 * 1024 * 1024

NT = (((1,), (1,)), ((), ()))
TN = (((0,), (0,)), ((), ()))
NN = (((1,), (0,)), ((), ()))


def dot(a, b, dims):
    return lax.dot_general(a, b, dims, preferred_element_type=F32)


def repeat_table():
    table = np.zeros((2, 144, NK), np.float32)
    for u in range(3):
        for v in range(3):
            for i in range(C):
                column = (3 * u + v) * C + i
                table[0, u * C + i, column] = 1.0
                table[1, v * C + i, column] = 1.0
    return jnp.asarray(table, BF16)


def position():
    return lax.axis_index("fold"), lax.axis_index("col")


def tile_of(fold_map, dilation):
    fold, col = position()
    slot = fold * 16 + col
    return fold_map[0, slot], fold_map[1, slot], dilation[0, 0], dilation[1, 0]


def place_of():
    col = position()[1]
    return col // 4, (col // 2) % 2, col % 2


def quad_kernel(own, core, xlo, both, out):
    out[0] = own[0]
    for k, block in enumerate((core, xlo, both)):
        out[1 + k] = block[...]


def fill_blocks(quad, z1, z2, z3, blocks):
    z, x, c = place_of()
    blocks[0] = jnp.full((C, B), OUTSIDE, F32)
    blocks[17] = jnp.full((C, B), OUTSIDE, F32)
    for step, got in ((0, quad), (1, z1), (2, z2), (3, z3)):
        there = 1 + (z ^ step) * 4
        for k in range(4):
            blocks[there + (x ^ (k // 2)) * 2 + (c ^ (k % 2))] = got[k].astype(F32)


def spread_lanes(blocks, tile, table, first, count):
    before, here, after = blocks[tile], blocks[tile + 1], blocks[tile + 2]
    for q in range(first - DMAX, first + count + DMAX):
        source, lane = (before, q + B) if q < 0 else ((here, q) if q < B else (after, q - B))
        table[q - first + DMAX] = jnp.broadcast_to(source[:, lane : lane + 1], (C, B)).astype(BF16)


def windows(blocks, tile, rate):
    lane = lax.broadcasted_iota(jnp.int32, (C, B), 1)
    before, here, after = blocks[tile], blocks[tile + 1], blocks[tile + 2]
    low = jnp.where(lane < rate, pltpu.roll(before, rate, 1), pltpu.roll(here, rate, 1))
    high = jnp.where(lane >= B - rate, pltpu.roll(after, B - rate, 1), pltpu.roll(here, B - rate, 1))
    return [low.astype(BF16), here.astype(BF16), high.astype(BF16)]


def scatter_back(grads, tile, rate, shifted):
    lane = lax.broadcasted_iota(jnp.int32, (C, B), 1)
    low, here, high = shifted
    low = pltpu.roll(low, B - rate, 1)
    high = pltpu.roll(high, rate, 1)
    zero = jnp.zeros((C, B), F32)
    grads[tile] += jnp.where(lane >= B - rate, low, zero)
    grads[tile + 2] += jnp.where(lane < rate, high, zero)
    grads[tile + 1] += (
        jnp.where(lane < B - rate, low, zero) + here + jnp.where(lane >= rate, high, zero)
    )


def store_rows(full, bias, first, stage32, count):
    for k in range(full.shape[1] // B):
        stage32[pl.ds(first + k, C, stride=count + PAD), :] = full[:, k * B : (k + 1) * B] + bias


def round_rows(stage32, stage, count):
    for c in range(C):
        stage[c] = stage32[c * (count + PAD) : c * (count + PAD) + count, :].astype(BF16)


def gradient_kernel(
    fold_map, dilation, quad, z1, z2, z3, weight, repeat, bias, cot, cols,
    send, keep, around, meta, pair_hbm,
    blocks, shift, minus, sums, grads, wgrad, table, rows, cot32, stage32, stage, sem,
):
    tile_i, tile_j, rate_r, rate_c = tile_of(fold_map, dilation)
    core_index = place_of()[2]
    fill_blocks(quad, z1, z2, z3, blocks)
    for k in range(3):
        around[k] = blocks[tile_i + k]
        around[3 + k] = blocks[tile_j + k]
    one, zero = jnp.ones((), BF16), jnp.zeros((), BF16)
    column = lax.broadcasted_iota(jnp.int32, (B, NK), 1)
    bias_mark = jnp.where(column == 432, 1.0, 0.0)
    grads[...] = jnp.zeros_like(grads)
    for k, value in enumerate((tile_i, tile_j, rate_r, rate_c)):
        meta[k] = value
    weight_wide = jnp.concatenate([weight[...].astype(F32), jnp.zeros((C, NK - 432), F32)], 1)
    empty = jnp.zeros((C, NK), F32)

    def tables(slot, tile, rate, which, mark):
        table = dot(jnp.concatenate(windows(blocks, tile, rate), 0), repeat[which], TN)
        minus[slot] = (-table).astype(BF16)
        shift[slot] = table + bias_mark if mark else table

    def back_sums(slot, tile, rate, which):
        tiles = []
        for at in range(NK // B):
            total = sums[slot, at, pl.ds(0, B, stride=8), :]
            for part in range(1, 8):
                total += sums[slot, at, pl.ds(part, B, stride=8), :]
            tiles.append(total)
        total = jnp.concatenate(tiles, 1)
        high = total.astype(BF16)
        low = (total - high.astype(F32)).astype(BF16)
        merged = dot(repeat[which], high, NT) + dot(repeat[which], low, NT)
        scatter_back(grads, tile, rate, [merged[k * C : (k + 1) * C] for k in range(3)])

    def loop(steps, start, first=0, last=B):
        def several(outer, carry):
            for inner in range(UNROLL):
                for step in steps:
                    carry = step(outer * UNROLL + inner, carry)
            return carry

        return lax.fori_loop(first // UNROLL, last // UNROLL, several, start)

    def take(slot, q, products, total):
        weighted = products * weight_wide
        partial = weighted[:8]
        for part in range(1, C // 8):
            partial += weighted[8 * part : 8 * part + 8]
        for at in range(NK // B):
            sums[slot, at, pl.ds(pl.multiple_of(q * 8, 8), 8), :] = partial[:, at * B : (at + 1) * B]
        return total + products * shift[slot, pl.ds(q, 1), :]

    def row_of(q):
        return rows[q]

    def col_of(q):
        return cols[q]

    def cotangent_here():
        for c in range(C):
            cot32[c * (B + PAD) : c * (B + PAD) + B, :] = cot[c].astype(F32)
        for q in range(B):
            rows[q] = cot32[pl.ds(q, C, stride=B + PAD), :].astype(BF16)

    @pl.when(tile_i < tile_j)
    def one_tile():
        spread_lanes(blocks, tile_i, table, 0, B)
        bias_now, weight_now = bias[...], weight[...]
        window = windows(blocks, tile_j, rate_c)

        def some(step, carry):
            parts = []
            for k in range(ROWS):
                at = [table[DMAX + step * ROWS + k + m * rate_r] for m in (-1, 0, 1)]
                taps = [jnp.maximum(at[u] + window[v], zero) for u in range(3) for v in range(3)]
                parts.append(jnp.concatenate(taps, 0))
            store_rows(dot(weight_now, jnp.concatenate(parts, 1), NN), bias_now, step * ROWS, stage32, B)
            return carry

        lax.fori_loop(0, B // ROWS, some, 0)
        round_rows(stage32, stage, B)
        save_pair = pltpu.make_async_copy(stage, pair_hbm, sem)
        save_pair.start()

        tables(0, tile_i, rate_r, 0, True)
        tables(1, tile_j, rate_c, 1, False)
        cotangent_here()

        def half(slot, other, grad_of):
            def step(q, total):
                at = jnp.broadcast_to(shift[slot, pl.ds(q, 1), :], (16, NK)).astype(BF16)
                at = jnp.concatenate([at] * (B // 16), 0)
                mask = jnp.where(at > minus[other], one, zero)
                return take(slot, q, dot(grad_of(q), mask, NN), total)

            return step

        wgrad[...] = loop([half(0, 1, row_of), half(1, 0, col_of)], empty)
        back_sums(0, tile_i, rate_r, 0)
        back_sums(1, tile_j, rate_c, 1)
        save_pair.wait()

    @pl.when(tile_i > tile_j)
    def two_triangles():
        tables(0, tile_i, rate_r, 0, True)
        tables(1, tile_i, rate_c, 1, False)
        tables(2, tile_j, rate_c, 1, True)
        tables(3, tile_j, rate_r, 0, False)
        cotangent_here()
        lane = lax.broadcasted_iota(jnp.int32, (C, B), 1).astype(BF16)

        def half(slot, other, grad_of, side, live):
            def step(q, total):
                at = jnp.broadcast_to(shift[slot, pl.ds(q, 1), :], (16, NK)).astype(BF16)
                at = jnp.concatenate([at] * ((live.stop - live.start) // 16), 0)
                mask = jnp.where(at > minus[other, live, :], one, zero)
                pads = [jnp.zeros((n, NK), BF16) for n in (live.start, B - live.stop)]
                mask = jnp.concatenate([x for x in (pads[0], mask, pads[1]) if x.shape[0]], 0)
                place = jnp.full((C, B), q, F32).astype(BF16)
                grad = jnp.where(side(lane, place), grad_of(q), zero)
                return take(slot, q, dot(grad, mask, NN), total)

            return step

        total = empty
        for part in range(PARTS):
            lines = (part * B // PARTS, (part + 1) * B // PARTS)
            after, before = slice(lines[0], B), slice(0, lines[1])
            total = loop(
                [
                    half(0, 1, row_of, lambda s, r: s >= r, after),
                    half(1, 0, col_of, lambda r, s: r <= s, before),
                    half(2, 3, row_of, lambda s, r: s < r, before),
                    half(3, 2, col_of, lambda r, s: r > s, after),
                ],
                total,
                *lines,
            )
        wgrad[...] = total
        back_sums(0, tile_i, rate_r, 0)
        back_sums(1, tile_i, rate_c, 1)
        back_sums(2, tile_j, rate_c, 1)
        back_sums(3, tile_j, rate_r, 0)

    for pair in range(8):
        send[pair] = grads[1 + 2 * pair + (1 - core_index)]
        keep[pair] = grads[1 + 2 * pair + core_index]
    total = wgrad[...]
    for part in range(4):
        piece = total[:, part * B : (part + 1) * B]
        send[8 + part] = piece
        keep[8 + part] = piece


def fold_kernel(
    first, count, meta, around, weight, bias, pair_before, after, pair_hbm, token,
    table_i, table_j, stage32, stage, sems,
):
    tile_i, tile_j, rate_r, rate_c = meta[0], meta[1], meta[2], meta[3]
    if token is not None:
        token[...] = jnp.zeros_like(token)

    @pl.when(tile_i > tile_j)
    def two_triangles():
        spread_lanes(around, 0, table_i, first, count)
        spread_lanes(around, 3, table_j, first, count)
        up_window, low_window = windows(around, 0, rate_c), windows(around, 3, rate_r)
        lane = lax.broadcasted_iota(jnp.int32, (C, B), 1).astype(BF16)
        weight_now, bias_now, zero = weight[...], bias[...], jnp.zeros((), BF16)
        saves = []
        for chunk in range(count // 16):
            parts = []
            for k in range(16):
                q = chunk * 16 + k
                upper = lane >= jnp.full((C, B), first + q, BF16)
                up = [table_i[DMAX + q + m * rate_r] for m in (-1, 0, 1)]
                low = [table_j[DMAX + q + m * rate_c] for m in (-1, 0, 1)]
                taps = [
                    jnp.where(upper, up[u] + up_window[v], low[v] + low_window[u])
                    for u in range(3)
                    for v in range(3)
                ]
                parts.append(jnp.concatenate([jnp.maximum(x, zero) for x in taps], 0))
            full = dot(weight_now, jnp.concatenate(parts, 1), NN)
            store_rows(full, bias_now, 0, stage32.at[chunk], 16)
            round_rows(stage32.at[chunk], stage.at[chunk], 16)
            here = pair_hbm.at[:, pl.ds(first + chunk * 16, 16), :]
            saves.append(pltpu.make_async_copy(stage.at[chunk], here, sems.at[chunk]))
            saves[-1].start()
        for save in saves:
            save.wait()


def shape(dims, kind):
    return jax.ShapeDtypeStruct(dims, kind)


SMEM = pl.BlockSpec(memory_space=pltpu.SMEM)
VMEM = pl.BlockSpec(memory_space=pltpu.VMEM)
ANY = pl.BlockSpec(memory_space=pl.ANY)
HBM = pl.BlockSpec(memory_space=pltpu.HBM)


def call(kernel, in_specs, out_shape, out_specs, scratch=(), aliases={}):
    return pl.pallas_call(
        kernel,
        out_shape=out_shape,
        in_specs=in_specs,
        out_specs=out_specs,
        scratch_shapes=list(scratch),
        input_output_aliases=aliases,
        compiler_params=pltpu.CompilerParams(vmem_limit_bytes=VMEM_BYTES),
    )


def gradients(fold_map, dilation, pieces, weight, bias, cot, cot_cols):
    return call(
        gradient_kernel,
        [SMEM, SMEM] + [VMEM] * 9,
        (
            shape((12, C, B), F32),
            shape((12, C, B), F32),
            shape((6, C, B), F32),
            shape((4,), jnp.int32),
            shape((C, B, B), BF16),
        ),
        (VMEM, VMEM, VMEM, SMEM, HBM),
        [
            pltpu.VMEM((18, C, B), F32),
            pltpu.VMEM((4, B, NK), F32),
            pltpu.VMEM((4, B, NK), BF16),
            pltpu.VMEM((4, NK // B, 8 * B, B), F32),
            pltpu.VMEM((18, C, B), F32),
            pltpu.VMEM((C, NK), F32),
            pltpu.VMEM((B + 2 * DMAX, C, B), BF16),
            pltpu.VMEM((B, C, B), BF16),
            pltpu.VMEM((C * (B + PAD), B), F32),
            pltpu.VMEM((C * (B + PAD), B), F32),
            pltpu.VMEM((C, B, B), BF16),
            pltpu.SemaphoreType.DMA,
        ],
    )(fold_map, dilation, *pieces, weight, repeat_table(), bias, cot, cot_cols)


def fold(which, meta, around, weight, bias, pair, after):
    first, count = PIECES[which]
    last = which == len(PIECES) - 1

    def kernel(*refs):
        fold_kernel(first, count, *refs[:7], *([None] if last else []), *refs[7:])

    done = call(
        kernel,
        [SMEM, VMEM, VMEM, VMEM, HBM, ANY],
        (shape((C, B, B), BF16),) + (() if last else (shape((8, B), F32),)),
        (HBM,) + (() if last else (VMEM,)),
        [
            pltpu.VMEM((count + 2 * DMAX, C, B), BF16),
            pltpu.VMEM((count + 2 * DMAX, C, B), BF16),
            pltpu.VMEM((count // 16, C * (16 + PAD), B), F32),
            pltpu.VMEM((count // 16, C, 16, B), BF16),
            pltpu.SemaphoreType.DMA((count // 16,)),
        ],
        {4: 0},
    )(meta, around, weight, bias, pair, after)
    return (done[0], None) if last else done


def after_core_kernel(keep, got, own, to1, to2, to3):
    z = place_of()[0]
    total = [(keep[k] + got[k]).astype(BF16) for k in range(8, 12)]
    for step, out in ((0, own), (1, to1), (2, to2), (3, to3)):
        first = (z ^ step) * 2
        for k in range(2):
            out[k] = (keep[first + k] + got[first + k]).astype(BF16)
        for k in range(4):
            out[2 + k] = total[k]


def sum4(own, a, b, c, k):
    return (own[k].astype(F32) + a[k].astype(F32)) + (b[k].astype(F32) + c[k].astype(F32))


def after_z_kernel(keep, a, b, c, token, own, other):
    x = place_of()[1]
    own[0] = sum4(keep, a, b, c, x).astype(BF16)
    other[0] = sum4(keep, a, b, c, 1 - x).astype(BF16)
    for k in range(4):
        total = sum4(keep, a, b, c, 2 + k).astype(BF16)
        own[1 + k] = total
        other[1 + k] = total


def after_x_kernel(keep, a, b, c, token, own):
    for k in range(5):
        own[k] = sum4(keep, a, b, c, k).astype(BF16)


def after_y_kernel(keep, a, b, c, grad_embed, grad_weight, grad_bias):
    grad_embed[...] = sum4(keep, a, b, c, 0) * (2048.0**-0.5)
    total = jnp.concatenate([sum4(keep, a, b, c, 1 + k) for k in range(4)], 1) * (1.0 / 2048.0)
    turned = total.T
    grad_weight[...] = turned[:432].reshape(9, C, C)
    grad_bias[...] = turned[432:433]


def body(bin_embed, conv_weight, conv_bias, dilation, fold_map, cotangent):
    fold_map, dilation = fold_map.T, jnp.broadcast_to(dilation[:, None], (2, B))

    def swap(value, fold_bits, col_bits):
        route = [
            (f * 16 + c, (f ^ fold_bits) * 16 + (c ^ col_bits)) for f in range(8) for c in range(16)
        ]
        return lax.ppermute(value, ("fold", "col"), route)

    core, xlo, both = swap(bin_embed, 0, 1), swap(bin_embed, 0, 2), swap(bin_embed, 0, 3)
    quad = call(quad_kernel, [VMEM] * 4, shape((4, C, B), BF16), VMEM)(
        jnp.broadcast_to(bin_embed[None], (2, C, B)), core, xlo, both
    )
    z1, z2, z3 = (swap(quad, 0, 4 * step) for step in (1, 2, 3))
    pieces = (quad, z1, z2, z3)

    cot = cotangent[0, 0]
    cot_cols = jnp.transpose(cot, (2, 0, 1))
    weight = jnp.transpose(conv_weight, (2, 0, 1)).reshape(C, 9 * C)
    bias = jnp.broadcast_to(conv_bias[:, None], (C, B))
    send, keep, around, meta, pair_out = gradients(
        fold_map, dilation, pieces, weight, bias, cot, cot_cols
    )

    def next_rows(which, pair_out, after):
        return fold(which, meta, around, weight, bias, pair_out, after)

    got = swap(send, 0, 1)
    half, part = shape((6, C, B), BF16), shape((5, C, B), BF16)
    keep, to1, to2, to3 = call(
        after_core_kernel, [VMEM, VMEM], (half,) * 4, (VMEM,) * 4
    )(keep, got)
    pair_out, token = next_rows(0, pair_out, keep)
    a, b, c = swap(to1, 0, 4), swap(to2, 0, 8), swap(to3, 0, 12)
    keep, other = call(
        after_z_kernel, [VMEM] * 4 + [ANY], (part, part), (VMEM, VMEM)
    )(keep, a, b, c, token)
    pair_out, token = next_rows(1, pair_out, keep)
    a, b, c = swap(other, 0, 2), swap(keep, 1, 0), swap(other, 1, 2)
    keep = call(after_x_kernel, [VMEM] * 4 + [ANY], part, VMEM)(keep, a, b, c, token)
    pair_out, token = next_rows(2, pair_out, keep)
    a, b, c = swap(keep, 2, 0), swap(keep, 4, 0), swap(keep, 6, 0)
    grad_embed, grad_weight, grad_bias = call(
        after_y_kernel,
        [VMEM] * 4,
        (shape((C, B), F32), shape((9, C, C), F32), shape((1, C), F32)),
        (VMEM,) * 3,
    )(keep, a, b, c)
    return pair_out[None, None], grad_embed, grad_weight, grad_bias.reshape(C)


def solution(mesh):
    placed = (P(None, "col"), P(), P(), P(), P(), P("fold", "col", None, None, None))
    return jax.shard_map(
        body,
        mesh=mesh,
        in_specs=placed,
        out_specs=(P("fold", "col", None, None, None), P(None, "col"), P(), P()),
        check_vma=False,
    )
```

```python
import functools

import jax
import jax.numpy as jnp
import numpy as np
from jax import lax
from jax.experimental import pallas as pl
from jax.experimental.pallas import tpu as pltpu
from jax.sharding import PartitionSpec as P

C = 48
B = 128
DMAX = 16
NK = 512
OUTSIDE = -16384.0
F32 = jnp.float32
BF16 = jnp.bfloat16
UNROLL = 16
PARTS = 4
ROWS = 32
PAD = 8
PIECES = ((0, 48), (48, 48), (96, 32))
VMEM_BYTES = 40 * 1024 * 1024

NT = (((1,), (1,)), ((), ()))
TN = (((0,), (0,)), ((), ()))
NN = (((1,), (0,)), ((), ()))


def dot(a, b, dims):
    return lax.dot_general(a, b, dims, preferred_element_type=F32)


def repeat_table():
    table = np.zeros((2, 144, NK), np.float32)
    for u in range(3):
        for v in range(3):
            for i in range(C):
                column = (3 * u + v) * C + i
                table[0, u * C + i, column] = 1.0
                table[1, v * C + i, column] = 1.0
    return jnp.asarray(table, BF16)


def position():
    return lax.axis_index("fold"), lax.axis_index("col")


def tile_of(fold_map, dilation):
    fold, col = position()
    slot = fold * 16 + col
    return fold_map[0, slot], fold_map[1, slot], dilation[0, 0], dilation[1, 0]


def place_of():
    col = position()[1]
    return col // 4, (col // 2) % 2, col % 2


def quad_kernel(own, core, xlo, both, out):
    out[0] = own[0]
    for k, block in enumerate((core, xlo, both)):
        out[1 + k] = block[...]


def fill_blocks(quad, z1, z2, z3, blocks):
    z, x, c = place_of()
    blocks[0] = jnp.full((C, B), OUTSIDE, F32)
    blocks[17] = jnp.full((C, B), OUTSIDE, F32)
    for step, got in ((0, quad), (1, z1), (2, z2), (3, z3)):
        there = 1 + (z ^ step) * 4
        for k in range(4):
            blocks[there + (x ^ (k // 2)) * 2 + (c ^ (k % 2))] = got[k].astype(F32)


def spread_lanes(blocks, tile, table, first, count):
    before, here, after = blocks[tile], blocks[tile + 1], blocks[tile + 2]
    for q in range(first - DMAX, first + count + DMAX):
        source, lane = (before, q + B) if q < 0 else ((here, q) if q < B else (after, q - B))
        table[q - first + DMAX] = jnp.broadcast_to(source[:, lane : lane + 1], (C, B)).astype(BF16)


def windows(blocks, tile, rate):
    lane = lax.broadcasted_iota(jnp.int32, (C, B), 1)
    before, here, after = blocks[tile], blocks[tile + 1], blocks[tile + 2]
    low = jnp.where(lane < rate, pltpu.roll(before, rate, 1), pltpu.roll(here, rate, 1))
    high = jnp.where(lane >= B - rate, pltpu.roll(after, B - rate, 1), pltpu.roll(here, B - rate, 1))
    return [low.astype(BF16), here.astype(BF16), high.astype(BF16)]


def scatter_back(grads, tile, rate, shifted):
    lane = lax.broadcasted_iota(jnp.int32, (C, B), 1)
    low, here, high = shifted
    low = pltpu.roll(low, B - rate, 1)
    high = pltpu.roll(high, rate, 1)
    zero = jnp.zeros((C, B), F32)
    grads[tile] += jnp.where(lane >= B - rate, low, zero)
    grads[tile + 2] += jnp.where(lane < rate, high, zero)
    grads[tile + 1] += (
        jnp.where(lane < B - rate, low, zero) + here + jnp.where(lane >= rate, high, zero)
    )


def store_rows(full, bias, first, stage32, count):
    for k in range(full.shape[1] // B):
        stage32[pl.ds(first + k, C, stride=count + PAD), :] = full[:, k * B : (k + 1) * B] + bias


def round_rows(stage32, stage, count):
    for c in range(C):
        stage[c] = stage32[c * (count + PAD) : c * (count + PAD) + count, :].astype(BF16)


def gradient_kernel(
    fold_map, dilation, quad, z1, z2, z3, weight, repeat, bias, cot, cols,
    send, keep, around, pair_hbm,
    blocks, shift, minus, sums, grads, wgrad, table, rows, cot32, stage32, stage, sem,
):
    tile_i, tile_j, rate_r, rate_c = tile_of(fold_map, dilation)
    core_index = place_of()[2]
    fill_blocks(quad, z1, z2, z3, blocks)
    for k in range(3):
        around[k] = blocks[tile_i + k]
        around[3 + k] = blocks[tile_j + k]
    one, zero = jnp.ones((), BF16), jnp.zeros((), BF16)
    column = lax.broadcasted_iota(jnp.int32, (B, NK), 1)
    bias_mark = jnp.where(column == 432, 1.0, 0.0)
    grads[...] = jnp.zeros_like(grads)
    weight_wide = jnp.concatenate([weight[...].astype(F32), jnp.zeros((C, NK - 432), F32)], 1)
    empty = jnp.zeros((C, NK), F32)

    def tables(slot, tile, rate, which, mark):
        table = dot(jnp.concatenate(windows(blocks, tile, rate), 0), repeat[which], TN)
        minus[slot] = (-table).astype(BF16)
        shift[slot] = table + bias_mark if mark else table

    def back_sums(slot, tile, rate, which):
        tiles = []
        for at in range(NK // B):
            total = sums[slot, at, pl.ds(0, B, stride=8), :]
            for part in range(1, 8):
                total += sums[slot, at, pl.ds(part, B, stride=8), :]
            tiles.append(total)
        total = jnp.concatenate(tiles, 1)
        high = total.astype(BF16)
        low = (total - high.astype(F32)).astype(BF16)
        merged = dot(repeat[which], high, NT) + dot(repeat[which], low, NT)
        scatter_back(grads, tile, rate, [merged[k * C : (k + 1) * C] for k in range(3)])

    def loop(steps, start, first=0, last=B):
        def several(outer, carry):
            for inner in range(UNROLL):
                for step in steps:
                    carry = step(outer * UNROLL + inner, carry)
            return carry

        return lax.fori_loop(first // UNROLL, last // UNROLL, several, start)

    def take(slot, q, products, total):
        weighted = products * weight_wide
        partial = weighted[:8]
        for part in range(1, C // 8):
            partial += weighted[8 * part : 8 * part + 8]
        for at in range(NK // B):
            sums[slot, at, pl.ds(pl.multiple_of(q * 8, 8), 8), :] = partial[:, at * B : (at + 1) * B]
        return total + products * shift[slot, pl.ds(q, 1), :]

    def row_of(q):
        return rows[q]

    def col_of(q):
        return cols[q]

    def cotangent_here():
        for c in range(C):
            cot32[c * (B + PAD) : c * (B + PAD) + B, :] = cot[c].astype(F32)
        for q in range(B):
            rows[q] = cot32[pl.ds(q, C, stride=B + PAD), :].astype(BF16)

    @pl.when(tile_i < tile_j)
    def one_tile():
        spread_lanes(blocks, tile_i, table, 0, B)
        bias_now, weight_now = bias[...], weight[...]
        window = windows(blocks, tile_j, rate_c)

        def some(step, carry):
            parts = []
            for k in range(ROWS):
                at = [table[DMAX + step * ROWS + k + m * rate_r] for m in (-1, 0, 1)]
                taps = [jnp.maximum(at[u] + window[v], zero) for u in range(3) for v in range(3)]
                parts.append(jnp.concatenate(taps, 0))
            store_rows(dot(weight_now, jnp.concatenate(parts, 1), NN), bias_now, step * ROWS, stage32, B)
            return carry

        lax.fori_loop(0, B // ROWS, some, 0)
        round_rows(stage32, stage, B)
        save_pair = pltpu.make_async_copy(stage, pair_hbm, sem)
        save_pair.start()

        tables(0, tile_i, rate_r, 0, True)
        tables(1, tile_j, rate_c, 1, False)
        cotangent_here()

        def half(slot, other, grad_of):
            def step(q, total):
                at = jnp.broadcast_to(shift[slot, pl.ds(q, 1), :], (16, NK)).astype(BF16)
                at = jnp.concatenate([at] * (B // 16), 0)
                mask = jnp.where(at > minus[other], one, zero)
                return take(slot, q, dot(grad_of(q), mask, NN), total)

            return step

        wgrad[...] = loop([half(0, 1, row_of), half(1, 0, col_of)], empty)
        back_sums(0, tile_i, rate_r, 0)
        back_sums(1, tile_j, rate_c, 1)
        save_pair.wait()

    @pl.when(tile_i > tile_j)
    def two_triangles():
        tables(0, tile_i, rate_r, 0, True)
        tables(1, tile_i, rate_c, 1, False)
        tables(2, tile_j, rate_c, 1, True)
        tables(3, tile_j, rate_r, 0, False)
        cotangent_here()
        lane = lax.broadcasted_iota(jnp.int32, (C, B), 1).astype(BF16)

        def half(slot, other, grad_of, side, live):
            def step(q, total):
                at = jnp.broadcast_to(shift[slot, pl.ds(q, 1), :], (16, NK)).astype(BF16)
                at = jnp.concatenate([at] * ((live.stop - live.start) // 16), 0)
                mask = jnp.where(at > minus[other, live, :], one, zero)
                pads = [jnp.zeros((n, NK), BF16) for n in (live.start, B - live.stop)]
                mask = jnp.concatenate([x for x in (pads[0], mask, pads[1]) if x.shape[0]], 0)
                place = jnp.full((C, B), q, F32).astype(BF16)
                grad = jnp.where(side(lane, place), grad_of(q), zero)
                return take(slot, q, dot(grad, mask, NN), total)

            return step

        total = empty
        for part in range(PARTS):
            lines = (part * B // PARTS, (part + 1) * B // PARTS)
            after, before = slice(lines[0], B), slice(0, lines[1])
            total = loop(
                [
                    half(0, 1, row_of, lambda s, r: s >= r, after),
                    half(1, 0, col_of, lambda r, s: r <= s, before),
                    half(2, 3, row_of, lambda s, r: s < r, before),
                    half(3, 2, col_of, lambda r, s: r > s, after),
                ],
                total,
                *lines,
            )
        wgrad[...] = total
        back_sums(0, tile_i, rate_r, 0)
        back_sums(1, tile_i, rate_c, 1)
        back_sums(2, tile_j, rate_c, 1)
        back_sums(3, tile_j, rate_r, 0)

    for pair in range(8):
        send[pair] = grads[1 + 2 * pair + (1 - core_index)]
        keep[pair] = grads[1 + 2 * pair + core_index]
    total = wgrad[...]
    for part in range(4):
        piece = total[:, part * B : (part + 1) * B]
        send[8 + part] = piece
        keep[8 + part] = piece


def fold_kernel(
    first, count, fold_map, dilation, around, weight, bias, pair_before, after, pair_hbm, token,
    table_i, table_j, stage32, stage, sems,
):
    tile_i, tile_j, rate_r, rate_c = tile_of(fold_map, dilation)
    if token is not None:
        token[...] = jnp.zeros_like(token)

    @pl.when(tile_i > tile_j)
    def two_triangles():
        spread_lanes(around, 0, table_i, first, count)
        spread_lanes(around, 3, table_j, first, count)
        up_window, low_window = windows(around, 0, rate_c), windows(around, 3, rate_r)
        lane = lax.broadcasted_iota(jnp.int32, (C, B), 1).astype(BF16)
        weight_now, bias_now, zero = weight[...], bias[...], jnp.zeros((), BF16)
        saves = []
        for chunk in range(count // 16):
            parts = []
            for k in range(16):
                q = chunk * 16 + k
                upper = lane >= jnp.full((C, B), first + q, BF16)
                up = [table_i[DMAX + q + m * rate_r] for m in (-1, 0, 1)]
                low = [table_j[DMAX + q + m * rate_c] for m in (-1, 0, 1)]
                taps = [
                    jnp.where(upper, up[u] + up_window[v], low[v] + low_window[u])
                    for u in range(3)
                    for v in range(3)
                ]
                parts.append(jnp.concatenate([jnp.maximum(x, zero) for x in taps], 0))
            full = dot(weight_now, jnp.concatenate(parts, 1), NN)
            store_rows(full, bias_now, 0, stage32.at[chunk], 16)
            round_rows(stage32.at[chunk], stage.at[chunk], 16)
            here = pair_hbm.at[:, pl.ds(first + chunk * 16, 16), :]
            saves.append(pltpu.make_async_copy(stage.at[chunk], here, sems.at[chunk]))
            saves[-1].start()
        for save in saves:
            save.wait()


def shape(dims, kind):
    return jax.ShapeDtypeStruct(dims, kind)


SMEM = pl.BlockSpec(memory_space=pltpu.SMEM)
VMEM = pl.BlockSpec(memory_space=pltpu.VMEM)
ANY = pl.BlockSpec(memory_space=pl.ANY)
HBM = pl.BlockSpec(memory_space=pltpu.HBM)


def call(kernel, in_specs, out_shape, out_specs, scratch=(), aliases={}):
    return pl.pallas_call(
        kernel,
        out_shape=out_shape,
        in_specs=in_specs,
        out_specs=out_specs,
        scratch_shapes=list(scratch),
        input_output_aliases=aliases,
        compiler_params=pltpu.CompilerParams(vmem_limit_bytes=VMEM_BYTES),
    )


def gradients(fold_map, dilation, pieces, weight, bias, cot, cot_cols):
    return call(
        gradient_kernel,
        [SMEM, SMEM] + [VMEM] * 9,
        (
            shape((12, C, B), F32),
            shape((12, C, B), F32),
            shape((6, C, B), F32),
            shape((C, B, B), BF16),
        ),
        (VMEM, VMEM, VMEM, HBM),
        [
            pltpu.VMEM((18, C, B), F32),
            pltpu.VMEM((4, B, NK), F32),
            pltpu.VMEM((4, B, NK), BF16),
            pltpu.VMEM((4, NK // B, 8 * B, B), F32),
            pltpu.VMEM((18, C, B), F32),
            pltpu.VMEM((C, NK), F32),
            pltpu.VMEM((B + 2 * DMAX, C, B), BF16),
            pltpu.VMEM((B, C, B), BF16),
            pltpu.VMEM((C * (B + PAD), B), F32),
            pltpu.VMEM((C * (B + PAD), B), F32),
            pltpu.VMEM((C, B, B), BF16),
            pltpu.SemaphoreType.DMA,
        ],
    )(fold_map, dilation, *pieces, weight, repeat_table(), bias, cot, cot_cols)


def fold(which, fold_map, dilation, around, weight, bias, pair, after):
    first, count = PIECES[which]
    last = which == len(PIECES) - 1

    def kernel(*refs):
        fold_kernel(first, count, *refs[:8], *([None] if last else []), *refs[8:])

    done = call(
        kernel,
        [SMEM, SMEM, VMEM, VMEM, VMEM, HBM, ANY],
        (shape((C, B, B), BF16),) + (() if last else (shape((8, B), F32),)),
        (HBM,) + (() if last else (VMEM,)),
        [
            pltpu.VMEM((count + 2 * DMAX, C, B), BF16),
            pltpu.VMEM((count + 2 * DMAX, C, B), BF16),
            pltpu.VMEM((count // 16, C * (16 + PAD), B), F32),
            pltpu.VMEM((count // 16, C, 16, B), BF16),
            pltpu.SemaphoreType.DMA((count // 16,)),
        ],
        {5: 0},
    )(fold_map, dilation, around, weight, bias, pair, after)
    return (done[0], None) if last else done


def after_core_kernel(keep, got, own, to1, to2, to3):
    z = place_of()[0]
    total = [(keep[k] + got[k]).astype(BF16) for k in range(8, 12)]
    for step, out in ((0, own), (1, to1), (2, to2), (3, to3)):
        first = (z ^ step) * 2
        for k in range(2):
            out[k] = (keep[first + k] + got[first + k]).astype(BF16)
        for k in range(4):
            out[2 + k] = total[k]


def sum4(own, a, b, c, k):
    return (own[k].astype(F32) + a[k].astype(F32)) + (b[k].astype(F32) + c[k].astype(F32))


def after_z_kernel(keep, a, b, c, token, own, other):
    x = place_of()[1]
    own[0] = sum4(keep, a, b, c, x).astype(BF16)
    other[0] = sum4(keep, a, b, c, 1 - x).astype(BF16)
    for k in range(4):
        total = sum4(keep, a, b, c, 2 + k).astype(BF16)
        own[1 + k] = total
        other[1 + k] = total


def after_x_kernel(keep, a, b, c, token, own):
    for k in range(5):
        own[k] = sum4(keep, a, b, c, k).astype(BF16)


def after_y_kernel(keep, a, b, c, grad_embed, grad_weight, grad_bias):
    grad_embed[...] = sum4(keep, a, b, c, 0) * (2048.0**-0.5)
    total = jnp.concatenate([sum4(keep, a, b, c, 1 + k) for k in range(4)], 1) * (1.0 / 2048.0)
    turned = total.T
    grad_weight[...] = turned[:432].reshape(9, C, C)
    grad_bias[...] = turned[432:433]


def body(bin_embed, conv_weight, conv_bias, dilation, fold_map, cotangent):
    fold_map, dilation = fold_map.T, jnp.broadcast_to(dilation[:, None], (2, B))

    def swap(value, fold_bits, col_bits):
        route = [
            (f * 16 + c, (f ^ fold_bits) * 16 + (c ^ col_bits)) for f in range(8) for c in range(16)
        ]
        return lax.ppermute(value, ("fold", "col"), route)

    core, xlo, both = swap(bin_embed, 0, 1), swap(bin_embed, 0, 2), swap(bin_embed, 0, 3)
    quad = call(quad_kernel, [VMEM] * 4, shape((4, C, B), BF16), VMEM)(
        jnp.broadcast_to(bin_embed[None], (2, C, B)), core, xlo, both
    )
    z1, z2, z3 = (swap(quad, 0, 4 * step) for step in (1, 2, 3))
    pieces = (quad, z1, z2, z3)

    cot = cotangent[0, 0]
    cot_cols = jnp.transpose(cot, (2, 0, 1))
    weight = jnp.transpose(conv_weight, (2, 0, 1)).reshape(C, 9 * C)
    bias = jnp.broadcast_to(conv_bias[:, None], (C, B))
    send, keep, around, pair_out = gradients(
        fold_map, dilation, pieces, weight, bias, cot, cot_cols
    )

    def next_rows(which, pair_out, after):
        return fold(which, fold_map, dilation, around, weight, bias, pair_out, after)

    got = swap(send, 0, 1)
    half, part = shape((6, C, B), BF16), shape((5, C, B), BF16)
    keep, to1, to2, to3 = call(
        after_core_kernel, [VMEM, VMEM], (half,) * 4, (VMEM,) * 4
    )(keep, got)
    pair_out, token = next_rows(0, pair_out, keep)
    a, b, c = swap(to1, 0, 4), swap(to2, 0, 8), swap(to3, 0, 12)
    keep, other = call(
        after_z_kernel, [VMEM] * 4 + [ANY], (part, part), (VMEM, VMEM)
    )(keep, a, b, c, token)
    pair_out, token = next_rows(1, pair_out, keep)
    a, b, c = swap(other, 0, 2), swap(keep, 1, 0), swap(other, 1, 2)
    keep = call(after_x_kernel, [VMEM] * 4 + [ANY], part, VMEM)(keep, a, b, c, token)
    pair_out, token = next_rows(2, pair_out, keep)
    a, b, c = swap(keep, 2, 0), swap(keep, 4, 0), swap(keep, 6, 0)
    grad_embed, grad_weight, grad_bias = call(
        after_y_kernel,
        [VMEM] * 4,
        (shape((C, B), F32), shape((9, C, C), F32), shape((1, C), F32)),
        (VMEM,) * 3,
    )(keep, a, b, c)
    return pair_out[None, None], grad_embed, grad_weight, grad_bias.reshape(C)


def solution(mesh):
    placed = (P(None, "col"), P(), P(), P(), P(), P("fold", "col", None, None, None))
    return jax.shard_map(
        body,
        mesh=mesh,
        in_specs=placed,
        out_specs=(P("fold", "col", None, None, None), P(None, "col"), P(), P()),
        check_vma=False,
    )
```
